512 devices in a mesh: tm: 16 (over y_lo, x, core), chan: 32 (over z, y_hi).
Axes of the slice: x: 4, y: 4 (y_hi: 2, y_lo: 2; y = y_hi * 2 + y_lo), z: 16, core: 2. Of those that a mesh axis runs over, the one named last changes fastest.
Arguments:
- record: float32 [16384, 4096], P('tm', 'chan'), may hold values from -6 to 6
- cuts: int32 [16, 1024], P('tm'), may hold values from 0 to 2048, as said below
Outputs:
- filtered: float32 [16384, 4096], P('tm', 'chan')
The draws below stay inside these ranges and needn't reach their ends.
Inputs may be any that keep to these rules, and one draw needn't show every extreme that they name: cuts[w, b] is the largest wavenumber magnitude kept in window w at frequency band b.
All inputs are finite; a program needn't handle non-finite values.
Results may differ from the reference program's by a relative error of at most 0.0003.
Values sent between devices are 32-bit elements; how exact they have to be, the bound alone decides.
A program may use at most 64 MiB of HBM per device.

```python
import math
import jax
import jax.numpy as jnp
from jax import lax

NCH = 4096
WIN = 2048
NWIN = 16
NT = 16384


def draw_cuts(key, part):
    key = jax.random.fold_in(key, 7)
    key_vals, key_top, key_low = jax.random.split(key, 3)
    total = NWIN * (WIN // 2)
    values = jax.random.randint(key_vals, (total,), 0, NCH // 2 + 1, dtype=jnp.int32)
    top_pos = jax.random.randint(key_top, (), 0, total, dtype=jnp.int32)
    low_pos = (top_pos + 1 + jax.random.randint(key_low, (), 0, total - 1, dtype=jnp.int32)) % total
    values = values.at[top_pos].set(NCH // 2).at[low_pos].set(0)
    return values.reshape(NWIN, WIN // 2)


def block_scale(stream_key, extent, shards, low, largest):
    def one(dim, blocks):
        heights = jax.random.uniform(jax.random.fold_in(jax.random.fold_in(stream_key, 6), dim), (blocks,), jnp.float32, low / len(shards), largest / len(shards))
        return jnp.repeat(jnp.exp(heights), extent[dim] // blocks).reshape((-1,) + (1,) * (len(extent) - dim - 1))

    gain = one(*shards[0])
    for cut in shards[1:]:
        gain = gain * one(*cut)
    return gain


def centred(key, dims, width, bound, cuts=(), kind=jnp.bfloat16):
    level = block_scale(key, dims, cuts, -0.22, 0.18) if cuts else 1.0
    array = jax.random.normal(key, dims, jnp.float32) * width * level
    return jnp.minimum(jnp.maximum(array, -bound), bound).astype(kind)


def setup_inputs(seed: int = 0) -> dict:
    arg_keys = jax.random.split(jax.random.key(seed), 3)
    record = centred(arg_keys[0], (NT, NCH), 1.0, 6.0, ((0, 16), (1, 32)), jnp.float32)
    cuts = draw_cuts(jax.random.fold_in(arg_keys[2], 71), 0)
    return {"record": record, "cuts": cuts}


def reference(record, cuts):
    hop = WIN // 2
    rim = hop // 2
    count = cuts.shape[0]
    taper = jnp.sin((math.pi / WIN) * jnp.arange(WIN, dtype=jnp.float32)) ** 2
    padded = jnp.pad(record, ((rim, rim), (0, 0)))
    freq = jnp.arange(WIN, dtype=jnp.int32)
    band = jnp.minimum(jnp.minimum(freq, WIN - freq), WIN // 2 - 1)
    wave = jnp.arange(NCH, dtype=jnp.int32)
    wave_abs = jnp.minimum(wave, NCH - wave)

    def one_window(index):
        segment = lax.dynamic_slice_in_dim(padded, index * hop, WIN, 0) * taper[:, None]
        spectrum = jnp.fft.fft2(segment)
        limits = jnp.take(cuts, index, axis=0)[band]
        keep = wave_abs[None, :] <= limits[:, None]
        result = jnp.real(jnp.fft.ifft2(jnp.where(keep, spectrum, 0.0)))
        return (result * taper[:, None]).astype(jnp.float32)

    windows = lax.map(one_window, jnp.arange(count, dtype=jnp.int32))
    summed = jnp.pad(windows[:, :hop], ((0, 1), (0, 0), (0, 0))) + jnp.pad(windows[:, hop:], ((1, 0), (0, 0), (0, 0)))
    summed = summed.reshape(-1, NCH)
    return summed[rim:rim + record.shape[0]]
```

```python
import functools
import math

import jax
import jax.numpy as jnp
import ml_dtypes
import numpy as np
from jax import lax
from jax.experimental import pallas as pl
from jax.experimental.pallas import tpu as pltpu
from jax.sharding import PartitionSpec as P

WIN = 2048
HOP = WIN // 2
RIM = HOP // 2
NCH = 4096
GROUPS = 32
LANES = 128
RING = 16
PARTS = 17
SUB = 1
CHUNKS = 2 * SUB
ROWS = 32 // SUB
BLOCK = 256
SPAN = HOP // SUB
FAR = 17
MESH_ID = pl.DeviceIdType.MESH


def split_bf16(table):
    high = table.astype(np.float32).astype(ml_dtypes.bfloat16)
    low = (table - high.astype(np.float64)).astype(ml_dtypes.bfloat16)
    return np.stack([high, low])


def cas(angle):
    return np.cos(angle) + np.sin(angle)


@functools.cache
def tables():
    index = np.arange(HOP)
    even = cas(2.0 * np.pi / HOP * (np.outer(index, index) % HOP))
    odd_index = 2 * index + 1
    odd = cas(2.0 * np.pi / (2 * WIN) * (np.outer(odd_index, odd_index) % (2 * WIN)))
    time = np.concatenate([split_bf16(even), split_bf16(odd)])
    taper = np.sin(np.pi / WIN * np.arange(WIN)) ** 2
    taper = np.repeat(taper[:, None], LANES, axis=1).astype(np.float32)
    lane = np.arange(LANES)
    angle = 2.0 * np.pi / LANES * (np.outer(lane, lane) % LANES)
    cosine, sine = np.cos(angle), np.sin(angle)
    forward = np.block([[cosine, -sine], [sine, cosine]])
    inverse = np.block([[cosine, sine], [-sine, cosine]])
    chan = np.concatenate([split_bf16(forward), split_bf16(inverse)])
    angle = 2.0 * np.pi / NCH * np.outer(np.arange(PARTS), lane)
    twist = np.stack([np.cos(angle), np.sin(angle)]).astype(np.float32)
    twist = np.repeat(twist[:, :, None, :], 8, axis=2)
    wave = np.arange(PARTS)[:, None] + GROUPS * lane[None, :]
    wave = np.minimum(wave, NCH - wave)
    wave = np.concatenate([wave, wave], axis=1).astype(np.int32)
    wave = np.repeat(wave[:, None, :], 8, axis=1)
    return time, taper, chan, twist, wave


def real_dft(x):
    n = len(x)
    if n == 1:
        return [(x[0], None)]
    if n == 2:
        return [(x[0] + x[1], None), (x[0] - x[1], None)]
    even = real_dft(x[0::2])
    odd = real_dft(x[1::2])
    half = n // 2
    out = [None] * (half + 1)
    out[0] = (even[0][0] + odd[0][0], None)
    out[half] = (even[0][0] - odd[0][0], None)
    for k in range(1, half // 2 + 1):
        e_re, e_im = even[k]
        o_re, o_im = odd[k]
        if 2 * k == half:
            out[k] = (e_re, -o_re)
            continue
        c, s = math.cos(2.0 * math.pi * k / n), math.sin(2.0 * math.pi * k / n)
        t_re = c * o_re + s * o_im
        t_im = c * o_im - s * o_re
        out[k] = (e_re + t_re, e_im + t_im)
        out[half - k] = (e_re - t_re, t_im - e_im)
    return out


def real_inverse(spec):
    half = len(spec) - 1
    n = 2 * half
    first, last = spec[0][0], spec[half][0]
    if n == 2:
        return [first + last, first - last]
    even = [None] * (half // 2 + 1)
    odd = [None] * (half // 2 + 1)
    even[0] = (first + last, None)
    odd[0] = (first - last, None)
    for k in range(1, half // 2 + 1):
        a_re, a_im = spec[k]
        if 2 * k == half:
            even[k] = (2.0 * a_re, None)
            odd[k] = (-2.0 * a_im, None)
            continue
        b_re, b_im = spec[half - k]
        even[k] = (a_re + b_re, a_im - b_im)
        d_re, d_im = a_re - b_re, a_im + b_im
        c, s = math.cos(2.0 * math.pi * k / n), math.sin(2.0 * math.pi * k / n)
        odd[k] = (c * d_re - s * d_im, c * d_im + s * d_re)
    y_even = real_inverse(even)
    y_odd = real_inverse(odd)
    out = []
    for a, b in zip(y_even, y_odd):
        out += [a, b]
    return out


def dot(a, b):
    return jnp.dot(a, b, preferred_element_type=jnp.float32)


def halves(x):
    high = x.astype(jnp.bfloat16)
    low = (x - high.astype(jnp.float32)).astype(jnp.bfloat16)
    return high, low


def table_product(x, high_table, low_table):
    high, low = halves(x)
    return dot(high, high_table) + dot(high, low_table) + dot(low, high_table)


def peer_of(step, zed, side):
    there = (zed + 7 * (step // 2)) % RING
    return 2 * there + (side + step) % 2


def body(
    record_hbm, cuts_hbm, time_hbm, taper_hbm, chan_hbm, twist_hbm, wave_hbm,
    out,
    record, cuts, time, taper, chan, twist, wave, below, above, pair, rhs, send, recv, spec, turned, back, part,
    part_odd, low_in, high_in, go_hold, ret_hold,
    load_sem, halo_send, halo_recv, spill_send, spill_recv, go_send, go_recv, ret_send, ret_recv,
    hold_recv, hold_send,
):
    me = lax.axis_index("chan")
    tm = lax.axis_index("tm")
    count = 16
    zed, side = me // 2, me % 2
    up = (tm + 1) % count
    down = (tm + count - 1) % count

    loads = [
        pltpu.make_async_copy(record_hbm, record, load_sem.at[0]),
        pltpu.make_async_copy(taper_hbm, taper, load_sem.at[1]),
    ]
    for i in range(4):
        loads.append(pltpu.make_async_copy(time_hbm.at[i], time.at[i], load_sem.at[2 + i]))
    loads += [
        pltpu.make_async_copy(cuts_hbm, cuts, load_sem.at[6]),
        pltpu.make_async_copy(chan_hbm, chan, load_sem.at[7]),
        pltpu.make_async_copy(twist_hbm, twist, load_sem.at[8]),
        pltpu.make_async_copy(wave_hbm, wave, load_sem.at[9]),
    ]
    for load in loads:
        load.start()

    barrier = pltpu.get_barrier_semaphore()
    for other in (up, down):
        pl.semaphore_signal(barrier, inc=1, device_id={"tm": other}, device_id_type=MESH_ID)

    @pl.loop(1, GROUPS)
    def _(step):
        pl.semaphore_signal(
            barrier, inc=1, device_id={"chan": peer_of(step, zed, side)}, device_id_type=MESH_ID
        )

    pl.semaphore_wait(barrier, GROUPS + 1)

    halos = [
        pltpu.make_async_remote_copy(
            src_ref=record_hbm.at[pl.ds(RIM, RIM)], dst_ref=below,
            send_sem=halo_send.at[0], recv_sem=halo_recv.at[0],
            device_id={"tm": up}, device_id_type=MESH_ID,
        ),
        pltpu.make_async_remote_copy(
            src_ref=record_hbm.at[pl.ds(0, RIM)], dst_ref=above,
            send_sem=halo_send.at[1], recv_sem=halo_recv.at[1],
            device_id={"tm": down}, device_id_type=MESH_ID,
        ),
    ]
    for halo in halos:
        halo.start()

    def block_copy(source, target, send_sem, recv_sem, peer):
        return pltpu.make_async_remote_copy(
            src_ref=source, dst_ref=target, send_sem=send_sem, recv_sem=recv_sem,
            device_id={"chan": peer}, device_id_type=MESH_ID,
        )

    relay = 2 * ((zed + RING - 4) % RING) + side
    origin = 2 * ((zed + 4) % RING) + side

    def exchange(source, target, hold, chunk, way, send_sem, recv_sem):
        far = peer_of(FAR, zed, side)
        block_copy(
            source.at[chunk, far], hold.at[chunk], send_sem.at[chunk],
            hold_recv.at[way, chunk], relay,
        ).start()

        for first, last in ((1, FAR), (FAR + 1, GROUPS)):
            @pl.loop(first, last)
            def _(step):
                peer = peer_of(step, zed, side)
                block_copy(
                    source.at[chunk, peer], target.at[chunk, me], send_sem.at[chunk],
                    recv_sem.at[chunk], peer,
                ).start()

        target[chunk, me] = source[chunk, me]

    def forward(target, hold, chunk, way, recv_sem):
        copy = block_copy(
            hold.at[chunk], target.at[chunk, origin], hold_send.at[way, chunk],
            recv_sem.at[chunk], peer_of(FAR, origin // 2, side),
        )
        pltpu.make_async_copy(hold.at[chunk], hold.at[chunk], hold_recv.at[way, chunk]).wait()
        copy.start()
        forwards.append(copy)

    forwards = []

    def all_of(buffer, chunk, sem):
        span = buffer.at[chunk, pl.ds(0, GROUPS - 1)]
        return pltpu.make_async_copy(span, span, sem.at[chunk])

    for load in loads[:2]:
        load.wait()
    for halo in halos:
        halo.wait_recv()

    keep_low = jnp.where(tm > 0, 1.0, 0.0).astype(jnp.float32)
    keep_high = jnp.where(tm < count - 1, 1.0, 0.0).astype(jnp.float32)

    @pl.loop(0, RIM // 64)
    def _(i):
        rows = pl.ds(pl.multiple_of(i * 64, 64), 64)
        upper = pl.ds(pl.multiple_of(RIM + i * 64, 64), 64)
        a = below[rows] * (taper[rows] * keep_low)
        b = record[upper] * taper[pl.ds(pl.multiple_of(HOP + i * 64, 64), 64)]
        c = record[rows] * taper[upper]
        d = above[rows] * (taper[pl.ds(pl.multiple_of(HOP + RIM + i * 64, 64), 64)] * keep_high)
        for where, first, second in ((rows, a, b), (upper, c, d)):
            high, low = halves(first + second)
            rhs[0, where, 0:LANES] = high
            rhs[0, where, LANES : 2 * LANES] = low
            high, low = halves(first - second)
            rhs[1, where, 0:LANES] = high
            rhs[1, where, LANES : 2 * LANES] = low

    def time_rows(parity, rows, first=0, span=HOP):
        cols = slice(first, first + span)
        wide = dot(time[2 * parity, rows, cols], rhs[parity, cols])
        tail = dot(time[2 * parity + 1, rows, cols], rhs[parity, cols, 0:LANES])
        return wide[:, 0:LANES] + wide[:, LANES : 2 * LANES] + tail

    for chunk in range(CHUNKS):
        parity, s = chunk // SUB, chunk % SUB
        if s == 0:
            loads[2 + 2 * parity].wait()
            loads[3 + 2 * parity].wait()

        @pl.loop(0, SPAN // BLOCK)
        def _(i):
            rows = pl.ds(pl.multiple_of(s * SPAN + i * BLOCK, BLOCK), BLOCK)
            cells = time_rows(parity, rows).reshape(BLOCK // ROWS, ROWS, LANES)
            send[chunk, pl.ds(i * (BLOCK // ROWS), BLOCK // ROWS)] = cells

        if chunk > 0:
            forward(recv, go_hold, chunk - 1, 0, go_recv)
        exchange(send, recv, go_hold, chunk, 0, go_send, go_recv)

    forward(recv, go_hold, CHUNKS - 1, 0, go_recv)
    for load in loads[6:]:
        load.wait()

    for chunk in range(CHUNKS):
        parity, s = chunk // SUB, chunk % SUB
        row = lax.broadcasted_iota(jnp.int32, (ROWS, 1), 0)
        freq = 2 * (SPAN * s + ROWS * me + row) + parity
        band = jnp.minimum(jnp.minimum(freq, WIN - freq), HOP - 1)
        limit = jnp.zeros((ROWS, LANES), jnp.int32)
        for i in range(HOP // LANES):
            here = i * LANES + lax.broadcasted_iota(jnp.int32, (ROWS, LANES), 1)
            limit = limit + jnp.where(here == band, cuts[0:1, i * LANES : (i + 1) * LANES], 0)
        limit = jnp.sum(limit, axis=1, keepdims=True)

        all_of(recv, chunk, go_recv).wait()

        @pl.loop(0, ROWS // 8)
        def _(i):
            rows = pl.ds(pl.multiple_of(i * 8, 8), 8)
            lines = real_dft([recv[chunk, d, rows] for d in range(GROUPS)])
            for p, (re, im) in enumerate(lines):
                if p == 0:
                    spec[p, rows, 0:LANES] = re
                    spec[p, rows, LANES : 2 * LANES] = jnp.zeros_like(re)
                elif im is None:
                    spec[p, rows, 0:LANES] = re * twist[0, p]
                    spec[p, rows, LANES : 2 * LANES] = -(re * twist[1, p])
                else:
                    c, sn = twist[0, p], twist[1, p]
                    spec[p, rows, 0:LANES] = re * c + im * sn
                    spec[p, rows, LANES : 2 * LANES] = im * c - re * sn

        lines = spec[...].reshape(PARTS * ROWS, 2 * LANES)
        values = table_product(lines, chan[0], chan[1]).reshape(PARTS, ROWS, 2 * LANES)
        kept = jnp.where(wave[:, 0:1] <= limit[None], values, 0.0)
        lines = kept.reshape(PARTS * ROWS, 2 * LANES)
        spec[...] = table_product(lines, chan[2], chan[3]).reshape(PARTS, ROWS, 2 * LANES)

        @pl.loop(0, ROWS // 8)
        def _(i):
            rows = pl.ds(pl.multiple_of(i * 8, 8), 8)
            lines = []
            for p in range(PARTS):
                re, im = spec[p, rows, 0:LANES], spec[p, rows, LANES : 2 * LANES]
                c, sn = twist[0, p], twist[1, p]
                if p == 0:
                    lines.append((re, None))
                elif p == PARTS - 1:
                    lines.append((re * c - im * sn, None))
                else:
                    lines.append((re * c - im * sn, im * c + re * sn))
            for d, value in enumerate(real_inverse(lines)):
                turned[chunk, d, rows] = value

        exchange(turned, back, ret_hold, chunk, 1, ret_send, ret_recv)
        forward(back, ret_hold, chunk, 1, ret_recv)

    scale = 1.0 / (WIN * NCH)
    totals = (part, part_odd)
    for chunk in range(CHUNKS):
        parity, s = chunk // SUB, chunk % SUB
        all_of(back, chunk, ret_recv).wait()

        @pl.loop(0, SPAN // BLOCK)
        def _(i):
            where = pl.ds(pl.multiple_of(s * SPAN + i * BLOCK, BLOCK), BLOCK)
            blocks = back[chunk, pl.ds(i * (BLOCK // ROWS), BLOCK // ROWS)]
            high, low = halves(blocks.reshape(BLOCK, LANES))
            rhs[parity, where, 0:LANES] = high
            rhs[parity, where, LANES : 2 * LANES] = low

        if chunk == CHUNKS - 1:
            break

        @pl.loop(0, HOP // BLOCK)
        def _(i):
            rows = pl.ds(pl.multiple_of(i * BLOCK, BLOCK), BLOCK)
            value = time_rows(parity, rows, s * SPAN, SPAN)
            totals[parity][rows] = value if s == 0 else totals[parity][rows] + value

    spills = []
    for i in range(HOP // BLOCK):
        here = slice(i * BLOCK, (i + 1) * BLOCK)
        odd = time_rows(1, here, (SUB - 1) * SPAN, SPAN)
        if SUB > 1:
            odd = odd + part_odd[here]
        even = part[here]
        first = (even + odd) * (taper[here] * scale)
        second = (even - odd) * (taper[HOP + i * BLOCK : HOP + (i + 1) * BLOCK] * scale)
        if i < RIM // BLOCK:
            rows = slice(i * BLOCK, (i + 1) * BLOCK)
            pair[0, rows] = first
            out[RIM + i * BLOCK : RIM + (i + 1) * BLOCK] = second
            source, target, other = pair.at[0, rows], low_in.at[rows], down
        else:
            rows = slice(i * BLOCK - RIM, (i + 1) * BLOCK - RIM)
            out[rows] = first
            pair[1, rows] = second
            source, target, other = pair.at[1, rows], high_in.at[rows], up
        spills.append(
            pltpu.make_async_remote_copy(
                src_ref=source, dst_ref=target,
                send_sem=spill_send.at[i], recv_sem=spill_recv.at[i],
                device_id={"tm": other}, device_id_type=MESH_ID,
            )
        )
        spills[-1].start()

    for i, spill in enumerate(spills):
        spill.wait_recv()
        if i < RIM // BLOCK:
            rows, base, extra, keep = slice(i * BLOCK, (i + 1) * BLOCK), RIM, low_in, keep_high
        else:
            rows, base, extra, keep = slice(i * BLOCK - RIM, (i + 1) * BLOCK - RIM), 0, high_in, keep_low
        here = slice(base + rows.start, base + rows.stop)
        out[here] = out[here] + extra[rows] * keep

    for chunk in range(CHUNKS):
        all_of(send, chunk, go_send).wait()
        all_of(turned, chunk, ret_send).wait()
    for copy in halos + spills + forwards:
        copy.wait_send()


def per_device(record, cuts):
    time, taper, chan, twist, wave = tables()
    vmem = pl.BlockSpec(memory_space=pltpu.VMEM)
    hbm = pl.BlockSpec(memory_space=pltpu.HBM)
    blocks = (CHUNKS, GROUPS, ROWS, LANES)
    dma = pltpu.SemaphoreType.DMA
    return pl.pallas_call(
        body,
        out_shape=jax.ShapeDtypeStruct(record.shape, jnp.float32),
        in_specs=[hbm] * 7,
        out_specs=vmem,
        scratch_shapes=[
            pltpu.VMEM(record.shape, jnp.float32),
            pltpu.VMEM(cuts.shape, jnp.int32),
            pltpu.VMEM(time.shape, jnp.bfloat16),
            pltpu.VMEM(taper.shape, jnp.float32),
            pltpu.VMEM(chan.shape, jnp.bfloat16),
            pltpu.VMEM(twist.shape, jnp.float32),
            pltpu.VMEM(wave.shape, jnp.int32),
            pltpu.VMEM((RIM, LANES), jnp.float32),
            pltpu.VMEM((RIM, LANES), jnp.float32),
            pltpu.VMEM((2, RIM, LANES), jnp.float32),
            pltpu.VMEM((2, HOP, 2 * LANES), jnp.bfloat16),
            pltpu.VMEM(blocks, jnp.float32),
            pltpu.VMEM(blocks, jnp.float32),
            pltpu.VMEM((PARTS, ROWS, 2 * LANES), jnp.float32),
            pltpu.VMEM(blocks, jnp.float32),
            pltpu.VMEM(blocks, jnp.float32),
            pltpu.VMEM((HOP, LANES), jnp.float32),
            pltpu.VMEM((HOP, LANES), jnp.float32),
            pltpu.VMEM((RIM, LANES), jnp.float32),
            pltpu.VMEM((RIM, LANES), jnp.float32),
            pltpu.VMEM((CHUNKS, ROWS, LANES), jnp.float32),
            pltpu.VMEM((CHUNKS, ROWS, LANES), jnp.float32),
            dma((10,)), dma((2,)), dma((2,)), dma((4,)), dma((4,)),
            dma((CHUNKS,)), dma((CHUNKS,)), dma((CHUNKS,)), dma((CHUNKS,)),
            dma((2, CHUNKS)), dma((2, CHUNKS)),
        ],
        compiler_params=pltpu.CompilerParams(
            collective_id=0, has_side_effects=True, vmem_limit_bytes=60 * 1024 * 1024
        ),
    )(record, cuts, time, taper, chan, twist, wave)


def solution(mesh):
    return jax.shard_map(
        per_device,
        mesh=mesh,
        in_specs=(P("tm", "chan"), P("tm", None)),
        out_specs=P("tm", "chan"),
        check_vma=False,
    )
```

```python
import functools
import math

import jax
import jax.numpy as jnp
import ml_dtypes
import numpy as np
from jax import lax
from jax.experimental import pallas as pl
from jax.experimental.pallas import tpu as pltpu
from jax.sharding import PartitionSpec as P

WIN = 2048
HOP = WIN // 2
RIM = HOP // 2
NCH = 4096
GROUPS = 32
LANES = 128
RING = 16
PARTS = 17
CHUNKS = 2
ROWS = 16
HALF = GROUPS // 2
BLOCK = 256
MESH_ID = pl.DeviceIdType.MESH


def split_bf16(table):
    high = table.astype(np.float32).astype(ml_dtypes.bfloat16)
    low = (table - high.astype(np.float64)).astype(ml_dtypes.bfloat16)
    return np.stack([high, low])


def cas(angle):
    return np.cos(angle) + np.sin(angle)


@functools.cache
def tables():
    index = np.arange(HOP)
    even = cas(2.0 * np.pi / HOP * (np.outer(index, index) % HOP))
    odd_index = 2 * index + 1
    odd = cas(2.0 * np.pi / (2 * WIN) * (np.outer(odd_index, odd_index) % (2 * WIN)))
    time = np.concatenate([split_bf16(even), split_bf16(odd)])
    taper = np.sin(np.pi / WIN * np.arange(WIN)) ** 2
    taper = np.repeat(taper[:, None], LANES, axis=1).astype(np.float32)
    lane = np.arange(LANES)
    angle = 2.0 * np.pi / LANES * (np.outer(lane, lane) % LANES)
    cosine, sine = np.cos(angle), np.sin(angle)
    forward = np.block([[cosine, -sine], [sine, cosine]])
    inverse = np.block([[cosine, sine], [-sine, cosine]])
    chan = np.concatenate([split_bf16(forward), split_bf16(inverse)])
    angle = 2.0 * np.pi / NCH * np.outer(np.arange(PARTS), lane)
    twist = np.stack([np.cos(angle), np.sin(angle)]).astype(np.float32)
    twist = np.repeat(twist[:, :, None, :], 8, axis=2)
    return time, taper, chan, twist


def real_dft(x):
    n = len(x)
    if n == 1:
        return [(x[0], None)]
    if n == 2:
        return [(x[0] + x[1], None), (x[0] - x[1], None)]
    even = real_dft(x[0::2])
    odd = real_dft(x[1::2])
    half = n // 2
    out = [None] * (half + 1)
    out[0] = (even[0][0] + odd[0][0], None)
    out[half] = (even[0][0] - odd[0][0], None)
    for k in range(1, half // 2 + 1):
        e_re, e_im = even[k]
        o_re, o_im = odd[k]
        if 2 * k == half:
            out[k] = (e_re, -o_re)
            continue
        c, s = math.cos(2.0 * math.pi * k / n), math.sin(2.0 * math.pi * k / n)
        t_re = c * o_re + s * o_im
        t_im = c * o_im - s * o_re
        out[k] = (e_re + t_re, e_im + t_im)
        out[half - k] = (e_re - t_re, t_im - e_im)
    return out


def real_inverse(spec):
    half = len(spec) - 1
    n = 2 * half
    first, last = spec[0][0], spec[half][0]
    if n == 2:
        return [first + last, first - last]
    even = [None] * (half // 2 + 1)
    odd = [None] * (half // 2 + 1)
    even[0] = (first + last, None)
    odd[0] = (first - last, None)
    for k in range(1, half // 2 + 1):
        a_re, a_im = spec[k]
        if 2 * k == half:
            even[k] = (2.0 * a_re, None)
            odd[k] = (-2.0 * a_im, None)
            continue
        b_re, b_im = spec[half - k]
        even[k] = (a_re + b_re, a_im - b_im)
        d_re, d_im = a_re - b_re, a_im + b_im
        c, s = math.cos(2.0 * math.pi * k / n), math.sin(2.0 * math.pi * k / n)
        odd[k] = (c * d_re - s * d_im, c * d_im + s * d_re)
    y_even = real_inverse(even)
    y_odd = real_inverse(odd)
    out = []
    for a, b in zip(y_even, y_odd):
        out += [a, b]
    return out


def dot(a, b):
    return jnp.dot(a, b, preferred_element_type=jnp.float32)


def halves(x):
    high = x.astype(jnp.bfloat16)
    low = (x - high.astype(jnp.float32)).astype(jnp.bfloat16)
    return high, low


def table_product(x, high_table, low_table):
    high, low = halves(x)
    return dot(high, high_table) + dot(high, low_table) + dot(low, high_table)


def body(
    record_hbm, cuts_hbm, time_hbm, taper_hbm, chan_hbm, twist_hbm,
    out,
    cuts, time, taper, chan, twist,
    stage, recv, spec, coef, block, below, above, limit, rhs, back_rhs, part,
    own, spill_low, spill_high, low_in, high_in, arrived, turned, stage_back,
    load_sem, cut_send, cut_sem,
    rows_send, rows_recv, ring_send, ring_recv, wave_send, wave_recv, halo_send, halo_recv,
    spill_send, spill_recv, lines_send, lines_recv, home_send, home_recv, last_send, last_recv,
):
    tm = lax.axis_index("tm")
    chan_index = lax.axis_index("chan")
    zed, side = chan_index // 2, chan_index % 2
    place = 2 * tm + side

    def in_plane(other):
        return {"tm": other // 2, "chan": 2 * zed + other % 2}

    def in_ring(other):
        return {"chan": 2 * other + side}

    up = (zed + 1) % RING
    down = (zed + RING - 1) % RING

    loads = [pltpu.make_async_copy(taper_hbm, taper, load_sem.at[0])]
    for i in range(4):
        loads.append(pltpu.make_async_copy(time_hbm.at[i], time.at[i], load_sem.at[1 + i]))
    loads += [
        pltpu.make_async_copy(chan_hbm, chan, load_sem.at[5]),
        pltpu.make_async_copy(twist_hbm, twist, load_sem.at[6]),
    ]

    def piece(other, chunk):
        return record_hbm.at[pl.ds(pl.multiple_of(32 * other + ROWS * chunk, ROWS), ROWS)]

    mine = [
        pltpu.make_async_copy(piece(place, c), stage.at[c, place], load_sem.at[7 + c])
        for c in range(CHUNKS)
    ]

    barrier = pltpu.get_barrier_semaphore()

    @pl.loop(1, GROUPS)
    def _(step):
        other = (place + 11 * step) % GROUPS
        pl.semaphore_signal(barrier, inc=1, device_id=in_plane(other), device_id_type=MESH_ID)

    @pl.loop(1, RING)
    def _(step):
        other = (zed + 7 * step) % RING
        pl.semaphore_signal(barrier, inc=1, device_id=in_ring(other), device_id_type=MESH_ID)

    for load in mine + loads:
        load.start()

    pl.semaphore_wait(barrier, GROUPS + RING - 2)

    def remote(source, target, send_sem, recv_sem, device):
        return pltpu.make_async_remote_copy(
            src_ref=source, dst_ref=target, send_sem=send_sem, recv_sem=recv_sem,
            device_id=device, device_id_type=MESH_ID,
        )

    def plane_exchange(source_of, target, send_sem, recv_sem):
        @pl.loop(1, GROUPS)
        def _(step):
            other = (place + 11 * step) % GROUPS
            remote(source_of(other), target, send_sem, recv_sem, in_plane(other)).start()

    def ring_exchange(source, target, chunk, send_sem, recv_sem):
        @pl.loop(1, RING)
        def _(step):
            other = (zed + 7 * step) % RING
            remote(
                source.at[chunk, pl.ds(2 * other, 2)], target.at[chunk, pl.ds(2 * zed, 2)],
                send_sem.at[chunk], recv_sem.at[chunk], in_ring(other),
            ).start()

        for i in range(2):
            target[chunk, 2 * zed + i] = source[chunk, 2 * zed + i]

    def bytes_of(buffer, count, sem):
        span = buffer.at[0, pl.ds(0, count)]
        return pltpu.make_async_copy(span, span, sem)

    def plane_wait(sem):
        bytes_of(recv, GROUPS - 1, sem).wait()

    def ring_wait(sem):
        bytes_of(recv, GROUPS - 2, sem).wait()

    for c in range(CHUNKS):
        plane_exchange(
            lambda other: piece(other, c), stage.at[c, place], rows_send.at[c], rows_recv.at[c]
        )

    @pl.when(tm == zed)
    def _():
        @pl.loop(1, RING)
        def _(step):
            other = (tm + step) % RING
            remote(cuts_hbm, cuts, cut_send.at[step], cut_sem.at[0], {"tm": other}).start()

        copy = pltpu.make_async_copy(cuts_hbm, cuts, cut_sem.at[1])
        copy.start()
        copy.wait()

    for c in range(CHUNKS):
        mine[c].wait()
        plane_wait(rows_recv.at[c])
        ring_exchange(stage, recv, c, ring_send, ring_recv)

    @pl.when(tm != zed)
    def _():
        remote(cuts_hbm, cuts, cut_send.at[0], cut_sem.at[0], {"tm": zed}).wait_recv()

    for parity in range(2):
        @pl.loop(0, HOP // 32)
        def _(j):
            row = lax.broadcasted_iota(jnp.int32, (32, 1), 0)
            freq = 2 * (32 * j + row) + parity
            band = jnp.minimum(jnp.minimum(freq, WIN - freq), HOP - 1)
            total = jnp.zeros((32, LANES), jnp.int32)
            for i in range(HOP // LANES):
                here = i * LANES + lax.broadcasted_iota(jnp.int32, (32, LANES), 1)
                total = total + jnp.where(here == band, cuts[0:1, i * LANES : (i + 1) * LANES], 0)
            total = jnp.sum(total, axis=1, keepdims=True)
            rows = pl.ds(pl.multiple_of(j * 32, 32), 32)
            limit[parity, rows] = jnp.broadcast_to(total, (32, LANES))

    for load in loads:
        load.wait()

    whole = 2 * LANES
    for c in range(CHUNKS):
        ring_wait(ring_recv.at[c])

        @pl.loop(0, ROWS // 8)
        def _(i):
            rows = pl.ds(pl.multiple_of(i * 8, 8), 8)
            lines = real_dft([recv[c, d, rows] for d in range(GROUPS)])
            for p, (re, im) in enumerate(lines):
                if p == 0:
                    spec[p, rows, 0:LANES] = re
                    spec[p, rows, LANES:whole] = jnp.zeros_like(re)
                elif im is None:
                    spec[p, rows, 0:LANES] = re * twist[0, p]
                    spec[p, rows, LANES:whole] = -(re * twist[1, p])
                else:
                    cosine, sine = twist[0, p], twist[1, p]
                    spec[p, rows, 0:LANES] = re * cosine + im * sine
                    spec[p, rows, LANES:whole] = im * cosine - re * sine

        lines = spec[...].reshape(PARTS * ROWS, whole)
        lines = table_product(lines, chan[0], chan[1]).reshape(PARTS, ROWS, whole)
        for p in range(PARTS):
            re, im = lines[p, :, 0:LANES], lines[p, :, LANES:whole]
            if p == 0:
                coef[c, 0] = re - im
            elif p == PARTS - 1:
                coef[c, GROUPS - 1] = re - im
            else:
                coef[c, 2 * p - 1] = re
                coef[c, 2 * p] = im

        plane_exchange(
            lambda other: coef.at[c, other], block.at[c, place], wave_send.at[c], wave_recv.at[c]
        )
        block[c, place] = coef[c, place]

    halos = []
    for c in range(CHUNKS):
        plane_wait(wave_recv.at[c])
        halos += [
            remote(
                block.at[c, pl.ds(HALF, HALF)], below.at[c],
                halo_send.at[2 * c], halo_recv.at[2 * c], in_ring(up),
            ),
            remote(
                block.at[c, pl.ds(0, HALF)], above.at[c],
                halo_send.at[2 * c + 1], halo_recv.at[2 * c + 1], in_ring(down),
            ),
        ]
        for halo in halos[-2:]:
            halo.start()

    keep_low = jnp.where(zed > 0, 1.0, 0.0).astype(jnp.float32)
    keep_high = jnp.where(zed < RING - 1, 1.0, 0.0).astype(jnp.float32)

    for c in range(CHUNKS):
        for halo in halos[2 * c : 2 * c + 2]:
            halo.wait_recv()

        @pl.loop(0, HALF)
        def _(q):
            def at(base):
                return pl.ds(pl.multiple_of(base + 32 * q + ROWS * c, ROWS), ROWS)

            first = below[c, q] * (taper[at(0)] * keep_low)
            second = block[c, HALF + q] * taper[at(HOP)]
            third = block[c, q] * taper[at(RIM)]
            fourth = above[c, q] * (taper[at(HOP + RIM)] * keep_high)
            for where, one, two in ((at(0), first, second), (at(RIM), third, fourth)):
                high, low = halves(one + two)
                rhs[0, where, 0:LANES] = high
                rhs[0, where, LANES:whole] = low
                high, low = halves(one - two)
                rhs[1, where, 0:LANES] = high
                rhs[1, where, LANES:whole] = low

    def time_rows(source, parity, rows):
        wide = dot(time[2 * parity, rows], source[parity])
        tail = dot(time[2 * parity + 1, rows], source[parity, :, 0:LANES])
        return wide[:, 0:LANES] + wide[:, LANES:whole] + tail

    lane = lax.broadcasted_iota(jnp.int32, (1, LANES), 1)
    wave = (place + 1) // 2 + GROUPS * lane
    wave = jnp.minimum(wave, NCH - wave)

    for parity in range(2):
        @pl.loop(0, HOP // BLOCK)
        def _(i):
            rows = pl.ds(pl.multiple_of(i * BLOCK, BLOCK), BLOCK)
            values = time_rows(rhs, parity, rows)
            high, low = halves(jnp.where(wave <= limit[parity, rows], values, 0.0))
            back_rhs[parity, rows, 0:LANES] = high
            back_rhs[parity, rows, LANES:whole] = low

    @pl.loop(0, HOP // BLOCK)
    def _(i):
        rows = pl.ds(pl.multiple_of(i * BLOCK, BLOCK), BLOCK)
        part[rows] = time_rows(back_rhs, 0, rows)

    scale = 1.0 / (WIN * NCH)
    pieces = BLOCK // ROWS
    spills = []
    for i in (2, 3, 0, 1):
        here = slice(i * BLOCK, (i + 1) * BLOCK)
        even = part[here]
        odd = time_rows(back_rhs, 1, here)
        first = (even + odd) * (taper[here] * scale)
        second = (even - odd) * (taper[HOP + i * BLOCK : HOP + (i + 1) * BLOCK] * scale)
        first = first.reshape(pieces, ROWS, LANES)
        second = second.reshape(pieces, ROWS, LANES)
        at = pl.ds(i % 2 * pieces, pieces)
        if i < 2:
            own[1, at] = second
            spill_low[at] = first
            source, target, other = spill_low.at[at], low_in.at[at], down
        else:
            own[0, at] = first
            spill_high[at] = second
            source, target, other = spill_high.at[at], high_in.at[at], up
        spills.append(remote(source, target, spill_send.at[i], spill_recv.at[i], in_ring(other)))
        spills[-1].start()

    for c in range(CHUNKS):
        for spill in spills[2 * c : 2 * c + 2]:
            spill.wait_recv()
        extra, keep = ((high_in, keep_low), (low_in, keep_high))[c]

        @pl.loop(0, GROUPS)
        def _(q):
            own[c, q] = own[c, q] + extra[q] * keep

        plane_exchange(
            lambda other: own.at[c, other], arrived.at[c, place], lines_send.at[c], lines_recv.at[c]
        )
        arrived[c, place] = own[c, place]

    for c in range(CHUNKS):
        plane_wait(lines_recv.at[c])
        for p in range(PARTS):
            if p == 0 or p == PARTS - 1:
                re = arrived[c, 0 if p == 0 else GROUPS - 1]
                im = -re
            else:
                re, im = arrived[c, 2 * p - 1], arrived[c, 2 * p]
            spec[p, :, 0:LANES] = re
            spec[p, :, LANES:whole] = im
        lines = spec[...].reshape(PARTS * ROWS, whole)
        spec[...] = table_product(lines, chan[2], chan[3]).reshape(PARTS, ROWS, whole)

        @pl.loop(0, ROWS // 8)
        def _(i):
            rows = pl.ds(pl.multiple_of(i * 8, 8), 8)
            lines = []
            for p in range(PARTS):
                re, im = spec[p, rows, 0:LANES], spec[p, rows, LANES:whole]
                cosine, sine = twist[0, p], twist[1, p]
                if p == 0:
                    lines.append((re, None))
                elif p == PARTS - 1:
                    lines.append((re * cosine - im * sine, None))
                else:
                    lines.append((re * cosine - im * sine, im * cosine + re * sine))
            for d, value in enumerate(real_inverse(lines)):
                turned[c, d, rows] = value

        ring_exchange(turned, stage_back, c, home_send, home_recv)

    def final(c):
        return pl.ds(pl.multiple_of(RIM * c + ROWS * place, ROWS), ROWS)

    for c in range(CHUNKS):
        ring_wait(home_recv.at[c])
        plane_exchange(
            lambda other: stage_back.at[c, other], out.at[final(c)], last_send.at[c], last_recv.at[c]
        )
        out[final(c)] = stage_back[c, place]

    for c in range(CHUNKS):
        plane_wait(last_recv.at[c])
    for c in range(CHUNKS):
        for sem in (rows_send, wave_send, lines_send, last_send):
            plane_wait(sem.at[c])
        for sem in (ring_send, home_send):
            ring_wait(sem.at[c])
    for copy in halos + spills:
        copy.wait_send()

    @pl.when(tm == zed)
    def _():
        @pl.loop(1, RING)
        def _(step):
            other = (tm + step) % RING
            remote(cuts_hbm, cuts, cut_send.at[step], cut_sem.at[0], {"tm": other}).wait_send()


def per_device(record, cuts):
    time, taper, chan, twist = tables()
    blocks = pltpu.VMEM((CHUNKS, GROUPS, ROWS, LANES), jnp.float32)
    half = pltpu.VMEM((CHUNKS, HALF, ROWS, LANES), jnp.float32)
    rim = pltpu.VMEM((GROUPS, ROWS, LANES), jnp.float32)
    sides = pltpu.VMEM((2, HOP, 2 * LANES), jnp.bfloat16)
    dma = pltpu.SemaphoreType.DMA
    return pl.pallas_call(
        body,
        out_shape=jax.ShapeDtypeStruct(record.shape, jnp.float32),
        in_specs=[pl.BlockSpec(memory_space=pltpu.HBM)] * 6,
        out_specs=pl.BlockSpec(memory_space=pltpu.VMEM),
        scratch_shapes=[
            pltpu.VMEM(cuts.shape, jnp.int32),
            pltpu.VMEM(time.shape, jnp.bfloat16),
            pltpu.VMEM(taper.shape, jnp.float32),
            pltpu.VMEM(chan.shape, jnp.bfloat16),
            pltpu.VMEM(twist.shape, jnp.float32),
            blocks, blocks,
            pltpu.VMEM((PARTS, ROWS, 2 * LANES), jnp.float32),
            blocks, blocks, half, half,
            pltpu.VMEM((2, HOP, LANES), jnp.int32),
            sides, sides,
            pltpu.VMEM((HOP, LANES), jnp.float32),
            blocks, rim, rim, rim, rim, blocks, blocks, blocks,
            dma((9,)), dma((RING,)), dma((2,)),
            dma((2,)), dma((2,)), dma((2,)), dma((2,)), dma((2,)), dma((2,)), dma((4,)), dma((4,)),
            dma((4,)), dma((4,)), dma((2,)), dma((2,)), dma((2,)), dma((2,)), dma((2,)), dma((2,)),
        ],
        compiler_params=pltpu.CompilerParams(
            collective_id=0, has_side_effects=True, vmem_limit_bytes=60 * 1024 * 1024
        ),
    )(record, cuts, time, taper, chan, twist)


def solution(mesh):
    return jax.shard_map(
        per_device,
        mesh=mesh,
        in_specs=(P("tm", "chan"), P("tm", None)),
        out_specs=P("tm", "chan"),
        check_vma=False,
    )
```

```python
import functools
import math

import jax
import jax.numpy as jnp
import ml_dtypes
import numpy as np
from jax import lax
from jax.experimental import pallas as pl
from jax.experimental.pallas import tpu as pltpu
from jax.sharding import PartitionSpec as P

WIN = 2048
HOP = WIN // 2
RIM = HOP // 2
NCH = 4096
GROUPS = 32
LANES = 128
RING = 16
PARTS = 17
CHUNKS = 4
ROWS = 32 // CHUNKS
HALF = GROUPS // 2
TALL = WIN // LANES
TIMES = TALL // 2
PER_CHUNK = 8 // CHUNKS
MESH_ID = pl.DeviceIdType.MESH


def split_bf16(table):
    high = table.astype(np.float32).astype(ml_dtypes.bfloat16)
    low = (table - high.astype(np.float64)).astype(ml_dtypes.bfloat16)
    return np.stack([high, low])


def cas(angle):
    return np.cos(angle) + np.sin(angle)


@functools.cache
def tables():
    point = np.arange(LANES)
    blocks = []
    for p in range(TIMES):
        freq = p + TALL * point
        angle = 2.0 * np.pi / WIN * (np.outer(freq, point) % WIN)
        cosine, sine = np.cos(angle), np.sin(angle)
        if p == 0:
            middle = 2.0 * np.pi / WIN * (np.outer(TIMES + freq, point) % WIN)
            none = np.zeros_like(angle)
            blocks.append(np.block([[cas(angle), none], [none, cas(middle)]]))
        else:
            blocks.append(np.block([[cosine, sine], [-sine, cosine]]))
    blocks = np.stack(blocks)
    time = np.stack([split_bf16(blocks), split_bf16(blocks.transpose(0, 2, 1))])
    taper = np.sin(np.pi / WIN * np.arange(WIN)) ** 2
    taper = np.repeat(taper[:, None], LANES, axis=1).astype(np.float32)
    lane = np.arange(LANES)
    angle = 2.0 * np.pi / LANES * (np.outer(lane, lane) % LANES)
    cosine, sine = np.cos(angle), np.sin(angle)
    forward = np.block([[cosine, -sine], [sine, cosine]])
    inverse = np.block([[cosine, sine], [-sine, cosine]])
    chan = np.concatenate([split_bf16(forward), split_bf16(inverse)])
    angle = 2.0 * np.pi / NCH * np.outer(np.arange(PARTS), lane)
    twist = np.stack([np.cos(angle), np.sin(angle)]).astype(np.float32)
    twist = np.repeat(twist[:, :, None, :], 8, axis=2)
    return time, taper, chan, twist


def real_dft(x):
    n = len(x)
    if n == 1:
        return [(x[0], None)]
    if n == 2:
        return [(x[0] + x[1], None), (x[0] - x[1], None)]
    even = real_dft(x[0::2])
    odd = real_dft(x[1::2])
    half = n // 2
    out = [None] * (half + 1)
    out[0] = (even[0][0] + odd[0][0], None)
    out[half] = (even[0][0] - odd[0][0], None)
    for k in range(1, half // 2 + 1):
        e_re, e_im = even[k]
        o_re, o_im = odd[k]
        if 2 * k == half:
            out[k] = (e_re, -o_re)
            continue
        c, s = math.cos(2.0 * math.pi * k / n), math.sin(2.0 * math.pi * k / n)
        t_re = c * o_re + s * o_im
        t_im = c * o_im - s * o_re
        out[k] = (e_re + t_re, e_im + t_im)
        out[half - k] = (e_re - t_re, t_im - e_im)
    return out


def real_inverse(spec):
    half = len(spec) - 1
    n = 2 * half
    first, last = spec[0][0], spec[half][0]
    if n == 2:
        return [first + last, first - last]
    even = [None] * (half // 2 + 1)
    odd = [None] * (half // 2 + 1)
    even[0] = (first + last, None)
    odd[0] = (first - last, None)
    for k in range(1, half // 2 + 1):
        a_re, a_im = spec[k]
        if 2 * k == half:
            even[k] = (2.0 * a_re, None)
            odd[k] = (-2.0 * a_im, None)
            continue
        b_re, b_im = spec[half - k]
        even[k] = (a_re + b_re, a_im - b_im)
        d_re, d_im = a_re - b_re, a_im + b_im
        c, s = math.cos(2.0 * math.pi * k / n), math.sin(2.0 * math.pi * k / n)
        odd[k] = (c * d_re - s * d_im, c * d_im + s * d_re)
    y_even = real_inverse(even)
    y_odd = real_inverse(odd)
    out = []
    for a, b in zip(y_even, y_odd):
        out += [a, b]
    return out


def dot(a, b):
    return jnp.dot(a, b, preferred_element_type=jnp.float32)


def halves(x):
    high = x.astype(jnp.bfloat16)
    low = (x - high.astype(jnp.float32)).astype(jnp.bfloat16)
    return high, low


def table_product(x, high_table, low_table):
    high, low = halves(x)
    return dot(high, high_table) + dot(high, low_table) + dot(low, high_table)


def div(a, b):
    return lax.div(a, jnp.int32(b))


def rem(a, b):
    return lax.rem(a, jnp.int32(b))


def body(
    record_hbm, cuts_hbm, time_hbm, taper_hbm, chan_hbm, twist_hbm,
    out,
    cuts, time, taper, chan, twist,
    stage, recv, spec, coef, block, below, above, limit, lines_time,
    own, spill_low, spill_high, low_in, high_in, arrived, turned, stage_back,
    load_sem, cut_send, cut_sem,
    rows_send, rows_recv, ring_send, ring_recv, wave_send, wave_recv, halo_send, halo_recv,
    spill_send, spill_recv, lines_send, lines_recv, home_send, home_recv, last_send, last_recv,
):
    tm = lax.axis_index("tm")
    chan_index = lax.axis_index("chan")
    zed, side = div(chan_index, 2), rem(chan_index, 2)
    place = 2 * tm + side

    def in_plane(other):
        return {"tm": div(other, 2), "chan": 2 * zed + rem(other, 2)}

    def in_ring(other):
        return {"chan": 2 * other + side}

    up = rem(zed + 1, RING)
    down = rem(zed + RING - 1, RING)

    loads = [pltpu.make_async_copy(taper_hbm, taper, load_sem.at[0])]
    loads += [
        pltpu.make_async_copy(chan_hbm, chan, load_sem.at[1]),
        pltpu.make_async_copy(twist_hbm, twist, load_sem.at[2]),
        pltpu.make_async_copy(time_hbm, time, load_sem.at[3]),
    ]

    def piece(other, chunk):
        return record_hbm.at[pl.ds(pl.multiple_of(32 * other + ROWS * chunk, ROWS), ROWS)]

    mine = [
        pltpu.make_async_copy(piece(place, c), stage.at[c, place], load_sem.at[4 + c])
        for c in range(CHUNKS)
    ]

    barrier = pltpu.get_barrier_semaphore()

    @pl.loop(1, GROUPS)
    def _(step):
        other = rem(place + 11 * step, GROUPS)
        pl.semaphore_signal(barrier, inc=1, device_id=in_plane(other), device_id_type=MESH_ID)

    @pl.loop(1, RING)
    def _(step):
        other = rem(zed + 7 * step, RING)
        pl.semaphore_signal(barrier, inc=1, device_id=in_ring(other), device_id_type=MESH_ID)

    for load in mine + loads:
        load.start()

    pl.semaphore_wait(barrier, GROUPS + RING - 2)

    def remote(source, target, send_sem, recv_sem, device):
        return pltpu.make_async_remote_copy(
            src_ref=source, dst_ref=target, send_sem=send_sem, recv_sem=recv_sem,
            device_id=device, device_id_type=MESH_ID,
        )

    def plane_exchange(source_of, target, send_sem, recv_sem):
        @pl.loop(1, GROUPS)
        def _(step):
            other = rem(place + 11 * step, GROUPS)
            remote(source_of(other), target, send_sem, recv_sem, in_plane(other)).start()

    def ring_exchange(source, target, chunk, send_sem, recv_sem):
        @pl.loop(1, RING)
        def _(step):
            other = rem(zed + 7 * step, RING)
            remote(
                source.at[chunk, pl.ds(2 * other, 2)], target.at[chunk, pl.ds(2 * zed, 2)],
                send_sem.at[chunk], recv_sem.at[chunk], in_ring(other),
            ).start()

        for i in range(2):
            target[chunk, 2 * zed + i] = source[chunk, 2 * zed + i]

    def bytes_of(buffer, count, sem):
        span = buffer.at[0, pl.ds(0, count)]
        return pltpu.make_async_copy(span, span, sem)

    def plane_wait(sem):
        bytes_of(recv, GROUPS - 1, sem).wait()

    def ring_wait(sem):
        bytes_of(recv, GROUPS - 2, sem).wait()

    for c in range(CHUNKS):
        plane_exchange(
            lambda other: piece(other, c), stage.at[c, place], rows_send.at[c], rows_recv.at[c]
        )

    @pl.when(tm == zed)
    def _():
        @pl.loop(1, RING)
        def _(step):
            other = rem(tm + step, RING)
            remote(cuts_hbm, cuts, cut_send.at[step], cut_sem.at[0], {"tm": other}).start()

        copy = pltpu.make_async_copy(cuts_hbm, cuts, cut_sem.at[1])
        copy.start()
        copy.wait()

    for c in range(CHUNKS):
        mine[c].wait()
        plane_wait(rows_recv.at[c])
        ring_exchange(stage, recv, c, ring_send, ring_recv)

    @pl.when(tm != zed)
    def _():
        remote(cuts_hbm, cuts, cut_send.at[0], cut_sem.at[0], {"tm": zed}).wait_recv()

    for p in range(TIMES):
        @pl.loop(0, 8)
        def _(j):
            row = 32 * j + lax.broadcasted_iota(jnp.int32, (32, 1), 0)
            if p == 0:
                freq = jnp.where(row < LANES, TALL * row, TALL * (row - LANES) + TIMES)
            else:
                freq = p + TALL * jnp.where(row < LANES, row, row - LANES)
            band = jnp.minimum(jnp.minimum(freq, WIN - freq), HOP - 1)
            total = jnp.zeros((32, LANES), jnp.int32)
            for i in range(HOP // LANES):
                here = i * LANES + lax.broadcasted_iota(jnp.int32, (32, LANES), 1)
                total = total + jnp.where(here == band, cuts[0:1, i * LANES : (i + 1) * LANES], 0)
            total = jnp.sum(total, axis=1, keepdims=True)
            rows = pl.ds(pl.multiple_of(j * 32, 32), 32)
            limit[p, rows] = jnp.broadcast_to(total, (32, LANES))

    for load in loads:
        load.wait()

    whole = 2 * LANES
    for c in range(CHUNKS):
        ring_wait(ring_recv.at[c])

        @pl.loop(0, ROWS // 8)
        def _(i):
            rows = pl.ds(pl.multiple_of(i * 8, 8), 8)
            lines = real_dft([recv[c, d, rows] for d in range(GROUPS)])
            for p, (re, im) in enumerate(lines):
                if p == 0:
                    spec[p, rows, 0:LANES] = re
                    spec[p, rows, LANES:whole] = jnp.zeros_like(re)
                elif im is None:
                    spec[p, rows, 0:LANES] = re * twist[0, p]
                    spec[p, rows, LANES:whole] = -(re * twist[1, p])
                else:
                    cosine, sine = twist[0, p], twist[1, p]
                    spec[p, rows, 0:LANES] = re * cosine + im * sine
                    spec[p, rows, LANES:whole] = im * cosine - re * sine

        lines = spec[...].reshape(PARTS * ROWS, whole)
        lines = table_product(lines, chan[0], chan[1]).reshape(PARTS, ROWS, whole)
        for p in range(PARTS):
            re, im = lines[p, :, 0:LANES], lines[p, :, LANES:whole]
            if p == 0:
                coef[c, 0] = re - im
            elif p == PARTS - 1:
                coef[c, GROUPS - 1] = re - im
            else:
                coef[c, 2 * p - 1] = re
                coef[c, 2 * p] = im

        plane_exchange(
            lambda other: coef.at[c, other], block.at[c, place], wave_send.at[c], wave_recv.at[c]
        )
        block[c, place] = coef[c, place]

    halos = []
    for c in range(CHUNKS):
        plane_wait(wave_recv.at[c])
        halos += [
            remote(
                block.at[c, pl.ds(HALF, HALF)], below.at[c],
                halo_send.at[2 * c], halo_recv.at[2 * c], in_ring(up),
            ),
            remote(
                block.at[c, pl.ds(0, HALF)], above.at[c],
                halo_send.at[2 * c + 1], halo_recv.at[2 * c + 1], in_ring(down),
            ),
        ]
        for halo in halos[-2:]:
            halo.start()

    keep_low = jnp.where(zed > 0, 1.0, 0.0).astype(jnp.float32)
    keep_high = jnp.where(zed < RING - 1, 1.0, 0.0).astype(jnp.float32)

    quarter = TALL // 4
    for c in range(CHUNKS):
        for halo in halos[2 * c : 2 * c + 2]:
            halo.wait_recv()

        @pl.loop(0, 4)
        def _(a):
            start = 32 * a + ROWS * c
            cells = []
            for i in range(TALL):
                weight = taper[pl.ds(pl.multiple_of(LANES * i + start, 8), ROWS)]
                if i < quarter:
                    cells.append(below[c, 4 * i + a] * (weight * keep_low))
                elif i < 3 * quarter:
                    cells.append(block[c, 4 * (i - quarter) + a] * weight)
                else:
                    cells.append(above[c, 4 * (i - 3 * quarter) + a] * (weight * keep_high))
            here = pl.ds(pl.multiple_of(start, 8), ROWS)
            there = pl.ds(pl.multiple_of(LANES + start, 8), ROWS)
            for p, (re, im) in enumerate(real_dft(cells)):
                if p == TIMES:
                    lines_time[0, there] = re
                else:
                    lines_time[p, here] = re
                    if p > 0:
                        lines_time[p, there] = im

    lane = lax.broadcasted_iota(jnp.int32, (1, LANES), 1)
    wave = div(place + 1, 2) + GROUPS * lane
    wave = jnp.minimum(wave, NCH - wave)

    def time_product(way, p, values):
        high, low = halves(values)
        wide = dot(time[way, 0, p], jnp.concatenate([high, low], axis=1))
        return wide[:, 0:LANES] + wide[:, LANES:whole] + dot(time[way, 1, p], high)

    for p in range(TIMES):
        values = time_product(0, p, lines_time[p])
        lines_time[p] = time_product(1, p, jnp.where(wave <= limit[p], values, 0.0))

    scale = 1.0 / (WIN * NCH)
    per = LANES // ROWS

    @pl.loop(0, per)
    def _(g):
        here = pl.ds(pl.multiple_of(ROWS * g, ROWS), ROWS)
        there = pl.ds(pl.multiple_of(LANES + ROWS * g, ROWS), ROWS)
        lines = [(lines_time[0, here], None)]
        for p in range(1, TIMES):
            lines.append((lines_time[p, here], lines_time[p, there]))
        lines.append((lines_time[0, there], None))
        for i, value in enumerate(real_inverse(lines)):
            weight = taper[pl.ds(pl.multiple_of(LANES * i + ROWS * g, ROWS), ROWS)]
            value = value * (weight * scale)
            if i < quarter:
                target, k = spill_low, i
            elif i < 3 * quarter:
                target, k = own, i - quarter
            else:
                target, k = spill_high, i - 3 * quarter
            target[k // PER_CHUNK, per * (k % PER_CHUNK) + g] = value

    spills = {}
    order = [c for pair in zip(range(CHUNKS // 2), range(CHUNKS // 2, CHUNKS)) for c in pair]
    for c in order:
        k = c % (CHUNKS // 2)
        if c < CHUNKS // 2:
            source, target, other = spill_high.at[k], high_in.at[k], up
        else:
            source, target, other = spill_low.at[k], low_in.at[k], down
        spills[c] = remote(source, target, spill_send.at[c], spill_recv.at[c], in_ring(other))
        spills[c].start()

    for c in order:
        spills[c].wait_recv()
        extra, keep = (high_in, keep_low) if c < CHUNKS // 2 else (low_in, keep_high)

        @pl.loop(0, GROUPS)
        def _(q):
            own[c, q] = own[c, q] + extra[c % (CHUNKS // 2), q] * keep

        plane_exchange(
            lambda other: own.at[c, other], arrived.at[c, place], lines_send.at[c], lines_recv.at[c]
        )
        arrived[c, place] = own[c, place]

    for c in order:
        plane_wait(lines_recv.at[c])
        for p in range(PARTS):
            if p == 0 or p == PARTS - 1:
                re = arrived[c, 0 if p == 0 else GROUPS - 1]
                im = -re
            else:
                re, im = arrived[c, 2 * p - 1], arrived[c, 2 * p]
            spec[p, :, 0:LANES] = re
            spec[p, :, LANES:whole] = im
        lines = spec[...].reshape(PARTS * ROWS, whole)
        spec[...] = table_product(lines, chan[2], chan[3]).reshape(PARTS, ROWS, whole)

        @pl.loop(0, ROWS // 8)
        def _(i):
            rows = pl.ds(pl.multiple_of(i * 8, 8), 8)
            lines = []
            for p in range(PARTS):
                re, im = spec[p, rows, 0:LANES], spec[p, rows, LANES:whole]
                cosine, sine = twist[0, p], twist[1, p]
                if p == 0:
                    lines.append((re, None))
                elif p == PARTS - 1:
                    lines.append((re * cosine - im * sine, None))
                else:
                    lines.append((re * cosine - im * sine, im * cosine + re * sine))
            for d, value in enumerate(real_inverse(lines)):
                turned[c, d, rows] = value

        ring_exchange(turned, stage_back, c, home_send, home_recv)

    def final(c):
        return pl.ds(pl.multiple_of(HOP // CHUNKS * c + ROWS * place, ROWS), ROWS)

    for c in order:
        ring_wait(home_recv.at[c])
        plane_exchange(
            lambda other: stage_back.at[c, other], out.at[final(c)], last_send.at[c], last_recv.at[c]
        )
        out[final(c)] = stage_back[c, place]

    for c in range(CHUNKS):
        plane_wait(last_recv.at[c])
    for c in range(CHUNKS):
        for sem in (rows_send, wave_send, lines_send, last_send):
            plane_wait(sem.at[c])
        for sem in (ring_send, home_send):
            ring_wait(sem.at[c])
    for copy in halos + list(spills.values()):
        copy.wait_send()

    @pl.when(tm == zed)
    def _():
        @pl.loop(1, RING)
        def _(step):
            other = rem(tm + step, RING)
            remote(cuts_hbm, cuts, cut_send.at[step], cut_sem.at[0], {"tm": other}).wait_send()


def per_device(record, cuts):
    time, taper, chan, twist = tables()
    blocks = pltpu.VMEM((CHUNKS, GROUPS, ROWS, LANES), jnp.float32)
    half = pltpu.VMEM((CHUNKS, HALF, ROWS, LANES), jnp.float32)
    rim = pltpu.VMEM((CHUNKS // 2, GROUPS, ROWS, LANES), jnp.float32)
    dma = pltpu.SemaphoreType.DMA
    return pl.pallas_call(
        body,
        out_shape=jax.ShapeDtypeStruct(record.shape, jnp.float32),
        in_specs=[pl.BlockSpec(memory_space=pltpu.HBM)] * 6,
        out_specs=pl.BlockSpec(memory_space=pltpu.VMEM),
        scratch_shapes=[
            pltpu.VMEM(cuts.shape, jnp.int32),
            pltpu.VMEM(time.shape, jnp.bfloat16),
            pltpu.VMEM(taper.shape, jnp.float32),
            pltpu.VMEM(chan.shape, jnp.bfloat16),
            pltpu.VMEM(twist.shape, jnp.float32),
            blocks, blocks,
            pltpu.VMEM((PARTS, ROWS, 2 * LANES), jnp.float32),
            blocks, blocks, half, half,
            pltpu.VMEM((TIMES, 2 * LANES, LANES), jnp.int32),
            pltpu.VMEM((TIMES, 2 * LANES, LANES), jnp.float32),
            blocks, rim, rim, rim, rim, blocks, blocks, blocks,
            dma((4 + CHUNKS,)), dma((RING,)), dma((2,)),
            *[dma((CHUNKS,))] * 6, *[dma((2 * CHUNKS,))] * 2, *[dma((CHUNKS,))] * 8,
        ],
        compiler_params=pltpu.CompilerParams(
            collective_id=0, has_side_effects=True, vmem_limit_bytes=60 * 1024 * 1024
        ),
    )(record, cuts, time, taper, chan, twist)


def solution(mesh):
    return jax.shard_map(
        per_device,
        mesh=mesh,
        in_specs=(P("tm", "chan"), P("tm", None)),
        out_specs=P("tm", "chan"),
        check_vma=False,
    )
```

```python
import functools
import math

import jax
import jax.numpy as jnp
import ml_dtypes
import numpy as np
from jax import lax
from jax.experimental import pallas as pl
from jax.experimental.pallas import tpu as pltpu
from jax.sharding import PartitionSpec as P

WIN = 2048
HOP = WIN // 2
RIM = HOP // 2
NCH = 4096
GROUPS = 32
LANES = 128
RING = 16
PARTS = 17
CHUNKS = 4
ROWS = 32 // CHUNKS
HALF = GROUPS // 2
TALL = WIN // LANES
TIMES = TALL // 2
PER_CHUNK = 8 // CHUNKS
MESH_ID = pl.DeviceIdType.MESH


def split_bf16(table):
    high = table.astype(np.float32).astype(ml_dtypes.bfloat16)
    low = (table - high.astype(np.float64)).astype(ml_dtypes.bfloat16)
    return np.stack([high, low])


def cas(angle):
    return np.cos(angle) + np.sin(angle)


@functools.cache
def tables():
    point = np.arange(LANES)
    blocks = []
    for p in range(TIMES):
        freq = p + TALL * point
        angle = 2.0 * np.pi / WIN * (np.outer(freq, point) % WIN)
        cosine, sine = np.cos(angle), np.sin(angle)
        if p == 0:
            middle = 2.0 * np.pi / WIN * (np.outer(TIMES + freq, point) % WIN)
            none = np.zeros_like(angle)
            blocks.append(np.block([[cas(angle), none], [none, cas(middle)]]))
        else:
            blocks.append(np.block([[cosine, sine], [-sine, cosine]]))
    blocks = np.stack(blocks)
    time = np.stack([split_bf16(blocks), split_bf16(blocks.transpose(0, 2, 1))])
    time = time.transpose(0, 2, 1, 3, 4).reshape(2, TIMES, 4 * LANES, 2 * LANES)
    taper = np.sin(np.pi / WIN * np.arange(WIN)) ** 2
    taper = np.repeat(taper[:, None], LANES, axis=1).astype(np.float32)
    lane = np.arange(LANES)
    angle = 2.0 * np.pi / LANES * (np.outer(lane, lane) % LANES)
    cosine, sine = np.cos(angle), np.sin(angle)
    forward = np.block([[cosine, -sine], [sine, cosine]])
    inverse = np.block([[cosine, sine], [-sine, cosine]])
    chan = np.concatenate([split_bf16(forward), split_bf16(inverse)])
    angle = 2.0 * np.pi / NCH * np.outer(np.arange(PARTS), lane)
    twist = np.stack([np.cos(angle), np.sin(angle)]).astype(np.float32)
    twist = np.repeat(twist[:, :, None, :], 8, axis=2)
    return time, taper, chan, twist


def real_dft(x):
    n = len(x)
    if n == 1:
        return [(x[0], None)]
    if n == 2:
        return [(x[0] + x[1], None), (x[0] - x[1], None)]
    even = real_dft(x[0::2])
    odd = real_dft(x[1::2])
    half = n // 2
    out = [None] * (half + 1)
    out[0] = (even[0][0] + odd[0][0], None)
    out[half] = (even[0][0] - odd[0][0], None)
    for k in range(1, half // 2 + 1):
        e_re, e_im = even[k]
        o_re, o_im = odd[k]
        if 2 * k == half:
            out[k] = (e_re, -o_re)
            continue
        c, s = math.cos(2.0 * math.pi * k / n), math.sin(2.0 * math.pi * k / n)
        t_re = c * o_re + s * o_im
        t_im = c * o_im - s * o_re
        out[k] = (e_re + t_re, e_im + t_im)
        out[half - k] = (e_re - t_re, t_im - e_im)
    return out


def real_inverse(spec):
    half = len(spec) - 1
    n = 2 * half
    first, last = spec[0][0], spec[half][0]
    if n == 2:
        return [first + last, first - last]
    even = [None] * (half // 2 + 1)
    odd = [None] * (half // 2 + 1)
    even[0] = (first + last, None)
    odd[0] = (first - last, None)
    for k in range(1, half // 2 + 1):
        a_re, a_im = spec[k]
        if 2 * k == half:
            even[k] = (2.0 * a_re, None)
            odd[k] = (-2.0 * a_im, None)
            continue
        b_re, b_im = spec[half - k]
        even[k] = (a_re + b_re, a_im - b_im)
        d_re, d_im = a_re - b_re, a_im + b_im
        c, s = math.cos(2.0 * math.pi * k / n), math.sin(2.0 * math.pi * k / n)
        odd[k] = (c * d_re - s * d_im, c * d_im + s * d_re)
    y_even = real_inverse(even)
    y_odd = real_inverse(odd)
    out = []
    for a, b in zip(y_even, y_odd):
        out += [a, b]
    return out


def dot(a, b):
    return jnp.dot(a, b, preferred_element_type=jnp.float32)


def halves(x):
    high = x.astype(jnp.bfloat16)
    low = (x - high.astype(jnp.float32)).astype(jnp.bfloat16)
    return high, low


def table_product(x, high_table, low_table):
    high, low = halves(x)
    return dot(high, high_table) + dot(high, low_table) + dot(low, high_table)


def div(a, b):
    return lax.div(a, jnp.int32(b))


def rem(a, b):
    return lax.rem(a, jnp.int32(b))


def body(
    record_hbm, cuts_hbm, time_hbm, taper_hbm, chan_hbm, twist_hbm,
    out,
    cuts, time, taper, chan, twist,
    stage, recv, spec, coef, block, below, above, limit, lines_time,
    own, spill_low, spill_high, low_in, high_in, arrived, turned, stage_back,
    load_sem, cut_send, cut_sem,
    rows_send, rows_recv, ring_send, ring_recv, wave_send, wave_recv, halo_send, halo_recv,
    spill_send, spill_recv, lines_send, lines_recv, home_send, home_recv, last_send, last_recv,
):
    tm = lax.axis_index("tm")
    chan_index = lax.axis_index("chan")
    zed, side = div(chan_index, 2), rem(chan_index, 2)
    place = 2 * tm + side

    def in_plane(other):
        return {"tm": div(other, 2), "chan": 2 * zed + rem(other, 2)}

    def in_ring(other):
        return {"chan": 2 * other + side}

    up = rem(zed + 1, RING)
    down = rem(zed + RING - 1, RING)

    loads = [pltpu.make_async_copy(taper_hbm, taper, load_sem.at[0])]
    loads += [
        pltpu.make_async_copy(chan_hbm, chan, load_sem.at[1]),
        pltpu.make_async_copy(twist_hbm, twist, load_sem.at[2]),
        pltpu.make_async_copy(time_hbm, time, load_sem.at[3]),
    ]

    def piece(other, chunk):
        return record_hbm.at[pl.ds(pl.multiple_of(32 * other + ROWS * chunk, ROWS), ROWS)]

    mine = [
        pltpu.make_async_copy(piece(place, c), stage.at[c, place], load_sem.at[4 + c])
        for c in range(CHUNKS)
    ]

    barrier = pltpu.get_barrier_semaphore()

    @pl.loop(1, GROUPS)
    def _(step):
        other = rem(place + 11 * step, GROUPS)
        pl.semaphore_signal(barrier, inc=1, device_id=in_plane(other), device_id_type=MESH_ID)

    @pl.loop(1, RING)
    def _(step):
        other = rem(zed + 7 * step, RING)
        pl.semaphore_signal(barrier, inc=1, device_id=in_ring(other), device_id_type=MESH_ID)

    for load in mine + loads:
        load.start()

    pl.semaphore_wait(barrier, GROUPS + RING - 2)

    def remote(source, target, send_sem, recv_sem, device):
        return pltpu.make_async_remote_copy(
            src_ref=source, dst_ref=target, send_sem=send_sem, recv_sem=recv_sem,
            device_id=device, device_id_type=MESH_ID,
        )

    def plane_exchange(source_of, target, send_sem, recv_sem):
        @pl.loop(1, GROUPS)
        def _(step):
            other = rem(place + 11 * step, GROUPS)
            remote(source_of(other), target, send_sem, recv_sem, in_plane(other)).start()

    def ring_exchange(source, target, chunk, send_sem, recv_sem):
        @pl.loop(1, RING)
        def _(step):
            other = rem(zed + 7 * step, RING)
            remote(
                source.at[chunk, pl.ds(2 * other, 2)], target.at[chunk, pl.ds(2 * zed, 2)],
                send_sem.at[chunk], recv_sem.at[chunk], in_ring(other),
            ).start()

        for i in range(2):
            target[chunk, 2 * zed + i] = source[chunk, 2 * zed + i]

    def bytes_of(buffer, count, sem):
        span = buffer.at[0, pl.ds(0, count)]
        return pltpu.make_async_copy(span, span, sem)

    def plane_wait(sem):
        bytes_of(recv, GROUPS - 1, sem).wait()

    def ring_wait(sem):
        bytes_of(recv, GROUPS - 2, sem).wait()

    for c in range(CHUNKS):
        plane_exchange(
            lambda other: piece(other, c), stage.at[c, place], rows_send.at[c], rows_recv.at[c]
        )

    @pl.when(tm == zed)
    def _():
        @pl.loop(1, RING)
        def _(step):
            other = rem(tm + step, RING)
            remote(cuts_hbm, cuts, cut_send.at[step], cut_sem.at[0], {"tm": other}).start()

        copy = pltpu.make_async_copy(cuts_hbm, cuts, cut_sem.at[1])
        copy.start()
        copy.wait()

    for c in range(CHUNKS):
        mine[c].wait()
        plane_wait(rows_recv.at[c])
        ring_exchange(stage, recv, c, ring_send, ring_recv)

    @pl.when(tm != zed)
    def _():
        remote(cuts_hbm, cuts, cut_send.at[0], cut_sem.at[0], {"tm": zed}).wait_recv()

    for p in range(TIMES):
        @pl.loop(0, 8)
        def _(j):
            row = 32 * j + lax.broadcasted_iota(jnp.int32, (32, 1), 0)
            if p == 0:
                freq = jnp.where(row < LANES, TALL * row, TALL * (row - LANES) + TIMES)
            else:
                freq = p + TALL * jnp.where(row < LANES, row, row - LANES)
            band = jnp.minimum(jnp.minimum(freq, WIN - freq), HOP - 1)
            total = jnp.zeros((32, LANES), jnp.int32)
            for i in range(HOP // LANES):
                here = i * LANES + lax.broadcasted_iota(jnp.int32, (32, LANES), 1)
                total = total + jnp.where(here == band, cuts[0:1, i * LANES : (i + 1) * LANES], 0)
            total = jnp.sum(total, axis=1, keepdims=True)
            rows = pl.ds(pl.multiple_of(j * 32, 32), 32)
            limit[p, rows] = jnp.broadcast_to(total, (32, LANES))

    for load in loads:
        load.wait()

    whole = 2 * LANES
    keep_low = jnp.where(zed > 0, 1.0, 0.0).astype(jnp.float32)
    keep_high = jnp.where(zed < RING - 1, 1.0, 0.0).astype(jnp.float32)

    halos = []

    def start_halo(c):
        plane_wait(wave_recv.at[c])
        halos.extend([
            remote(
                block.at[c, pl.ds(HALF, HALF)], below.at[c],
                halo_send.at[2 * c], halo_recv.at[2 * c], in_ring(up),
            ),
            remote(
                block.at[c, pl.ds(0, HALF)], above.at[c],
                halo_send.at[2 * c + 1], halo_recv.at[2 * c + 1], in_ring(down),
            ),
        ])
        for halo in halos[-2:]:
            halo.start()

    quarter = TALL // 4

    def fold(c):
        for halo in halos[2 * c : 2 * c + 2]:
            halo.wait_recv()

        @pl.loop(0, 4)
        def _(a):
            start = 32 * a + ROWS * c
            cells = []
            for i in range(TALL):
                weight = taper[pl.ds(pl.multiple_of(LANES * i + start, 8), ROWS)]
                if i < quarter:
                    cells.append(below[c, 4 * i + a] * (weight * keep_low))
                elif i < 3 * quarter:
                    cells.append(block[c, 4 * (i - quarter) + a] * weight)
                else:
                    cells.append(above[c, 4 * (i - 3 * quarter) + a] * (weight * keep_high))
            here = pl.ds(pl.multiple_of(start, 8), ROWS)
            there = pl.ds(pl.multiple_of(LANES + start, 8), ROWS)
            for p, (re, im) in enumerate(real_dft(cells)):
                if p == TIMES:
                    lines_time[0, there] = re
                else:
                    lines_time[p, here] = re
                    if p > 0:
                        lines_time[p, there] = im

    for c in range(CHUNKS):
        ring_wait(ring_recv.at[c])

        @pl.loop(0, ROWS // 8)
        def _(i):
            rows = pl.ds(pl.multiple_of(i * 8, 8), 8)
            lines = real_dft([recv[c, d, rows] for d in range(GROUPS)])
            for p, (re, im) in enumerate(lines):
                if p == 0:
                    spec[p, rows, 0:LANES] = re
                    spec[p, rows, LANES:whole] = jnp.zeros_like(re)
                elif im is None:
                    spec[p, rows, 0:LANES] = re * twist[0, p]
                    spec[p, rows, LANES:whole] = -(re * twist[1, p])
                else:
                    cosine, sine = twist[0, p], twist[1, p]
                    spec[p, rows, 0:LANES] = re * cosine + im * sine
                    spec[p, rows, LANES:whole] = im * cosine - re * sine

        lines = spec[...].reshape(PARTS * ROWS, whole)
        lines = table_product(lines, chan[0], chan[1]).reshape(PARTS, ROWS, whole)
        for p in range(PARTS):
            re, im = lines[p, :, 0:LANES], lines[p, :, LANES:whole]
            if p == 0:
                coef[c, 0] = re - im
            elif p == PARTS - 1:
                coef[c, GROUPS - 1] = re - im
            else:
                coef[c, 2 * p - 1] = re
                coef[c, 2 * p] = im

        plane_exchange(
            lambda other: coef.at[c, other], block.at[c, place], wave_send.at[c], wave_recv.at[c]
        )
        block[c, place] = coef[c, place]
        if c > 0:
            start_halo(c - 1)
        if c > 1:
            fold(c - 2)

    start_halo(CHUNKS - 1)
    fold(CHUNKS - 2)
    fold(CHUNKS - 1)

    lane = lax.broadcasted_iota(jnp.int32, (1, LANES), 1)
    wave = div(place + 1, 2) + GROUPS * lane
    wave = jnp.minimum(wave, NCH - wave)

    def time_product(way, p, values):
        high, low = halves(values)
        wide = dot(time[way, p], jnp.concatenate([high, low], axis=1))
        main, rest = wide[0:whole], wide[whole : 2 * whole]
        return (main[:, LANES:whole] + rest[:, 0:LANES]) + (rest[:, LANES:whole] + main[:, 0:LANES])

    for p in range(TIMES):
        values = time_product(0, p, lines_time[p])
        lines_time[p] = time_product(1, p, jnp.where(wave <= limit[p], values, 0.0))

    scale = 1.0 / (WIN * NCH)
    per = LANES // ROWS

    @pl.loop(0, per)
    def _(g):
        here = pl.ds(pl.multiple_of(ROWS * g, ROWS), ROWS)
        there = pl.ds(pl.multiple_of(LANES + ROWS * g, ROWS), ROWS)
        lines = [(lines_time[0, here], None)]
        for p in range(1, TIMES):
            lines.append((lines_time[p, here], lines_time[p, there]))
        lines.append((lines_time[0, there], None))
        for i, value in enumerate(real_inverse(lines)):
            weight = taper[pl.ds(pl.multiple_of(LANES * i + ROWS * g, ROWS), ROWS)]
            value = value * (weight * scale)
            if i < quarter:
                target, k = spill_low, i
            elif i < 3 * quarter:
                target, k = own, i - quarter
            else:
                target, k = spill_high, i - 3 * quarter
            target[k // PER_CHUNK, per * (k % PER_CHUNK) + g] = value

    spills = {}
    order = [c for pair in zip(range(CHUNKS // 2), range(CHUNKS // 2, CHUNKS)) for c in pair]
    for c in order:
        k = c % (CHUNKS // 2)
        if c < CHUNKS // 2:
            source, target, other = spill_high.at[k], high_in.at[k], up
        else:
            source, target, other = spill_low.at[k], low_in.at[k], down
        spills[c] = remote(source, target, spill_send.at[c], spill_recv.at[c], in_ring(other))
        spills[c].start()

    def send_lines(c):
        spills[c].wait_recv()
        extra, keep = (high_in, keep_low) if c < CHUNKS // 2 else (low_in, keep_high)

        @pl.loop(0, GROUPS)
        def _(q):
            own[c, q] = own[c, q] + extra[c % (CHUNKS // 2), q] * keep

        plane_exchange(
            lambda other: own.at[c, other], arrived.at[c, place], lines_send.at[c], lines_recv.at[c]
        )
        arrived[c, place] = own[c, place]

    send_lines(order[0])
    for step, c in enumerate(order):
        if step + 1 < CHUNKS:
            send_lines(order[step + 1])
        plane_wait(lines_recv.at[c])
        for p in range(PARTS):
            if p == 0 or p == PARTS - 1:
                re = arrived[c, 0 if p == 0 else GROUPS - 1]
                im = -re
            else:
                re, im = arrived[c, 2 * p - 1], arrived[c, 2 * p]
            spec[p, :, 0:LANES] = re
            spec[p, :, LANES:whole] = im
        lines = spec[...].reshape(PARTS * ROWS, whole)
        spec[...] = table_product(lines, chan[2], chan[3]).reshape(PARTS, ROWS, whole)

        @pl.loop(0, ROWS // 8)
        def _(i):
            rows = pl.ds(pl.multiple_of(i * 8, 8), 8)
            lines = []
            for p in range(PARTS):
                re, im = spec[p, rows, 0:LANES], spec[p, rows, LANES:whole]
                cosine, sine = twist[0, p], twist[1, p]
                if p == 0:
                    lines.append((re, None))
                elif p == PARTS - 1:
                    lines.append((re * cosine - im * sine, None))
                else:
                    lines.append((re * cosine - im * sine, im * cosine + re * sine))
            for d, value in enumerate(real_inverse(lines)):
                turned[c, d, rows] = value

        ring_exchange(turned, stage_back, c, home_send, home_recv)

    def final(c):
        return pl.ds(pl.multiple_of(HOP // CHUNKS * c + ROWS * place, ROWS), ROWS)

    for c in order:
        ring_wait(home_recv.at[c])
        plane_exchange(
            lambda other: stage_back.at[c, other], out.at[final(c)], last_send.at[c], last_recv.at[c]
        )
        out[final(c)] = stage_back[c, place]

    for c in range(CHUNKS):
        plane_wait(last_recv.at[c])
    for c in range(CHUNKS):
        for sem in (rows_send, wave_send, lines_send, last_send):
            plane_wait(sem.at[c])
        for sem in (ring_send, home_send):
            ring_wait(sem.at[c])
    for copy in halos + list(spills.values()):
        copy.wait_send()

    @pl.when(tm == zed)
    def _():
        @pl.loop(1, RING)
        def _(step):
            other = rem(tm + step, RING)
            remote(cuts_hbm, cuts, cut_send.at[step], cut_sem.at[0], {"tm": other}).wait_send()


def per_device(record, cuts):
    time, taper, chan, twist = tables()
    blocks = pltpu.VMEM((CHUNKS, GROUPS, ROWS, LANES), jnp.float32)
    half = pltpu.VMEM((CHUNKS, HALF, ROWS, LANES), jnp.float32)
    rim = pltpu.VMEM((CHUNKS // 2, GROUPS, ROWS, LANES), jnp.float32)
    dma = pltpu.SemaphoreType.DMA
    return pl.pallas_call(
        body,
        out_shape=jax.ShapeDtypeStruct(record.shape, jnp.float32),
        in_specs=[pl.BlockSpec(memory_space=pltpu.HBM)] * 6,
        out_specs=pl.BlockSpec(memory_space=pltpu.VMEM),
        scratch_shapes=[
            pltpu.VMEM(cuts.shape, jnp.int32),
            pltpu.VMEM(time.shape, jnp.bfloat16),
            pltpu.VMEM(taper.shape, jnp.float32),
            pltpu.VMEM(chan.shape, jnp.bfloat16),
            pltpu.VMEM(twist.shape, jnp.float32),
            blocks, blocks,
            pltpu.VMEM((PARTS, ROWS, 2 * LANES), jnp.float32),
            blocks, blocks, half, half,
            pltpu.VMEM((TIMES, 2 * LANES, LANES), jnp.int32),
            pltpu.VMEM((TIMES, 2 * LANES, LANES), jnp.float32),
            blocks, rim, rim, rim, rim, blocks, blocks, blocks,
            dma((4 + CHUNKS,)), dma((RING,)), dma((2,)),
            *[dma((CHUNKS,))] * 6, *[dma((2 * CHUNKS,))] * 2, *[dma((CHUNKS,))] * 8,
        ],
        compiler_params=pltpu.CompilerParams(
            collective_id=0, has_side_effects=True, vmem_limit_bytes=60 * 1024 * 1024
        ),
    )(record, cuts, time, taper, chan, twist)


def solution(mesh):
    return jax.shard_map(
        per_device,
        mesh=mesh,
        in_specs=(P("tm", "chan"), P("tm", None)),
        out_specs=P("tm", "chan"),
        check_vma=False,
    )
```

```python
import functools
import math

import jax
import jax.numpy as jnp
import ml_dtypes
import numpy as np
from jax import lax
from jax.experimental import pallas as pl
from jax.experimental.pallas import tpu as pltpu
from jax.sharding import PartitionSpec as P

WIN = 2048
HOP = WIN // 2
RIM = HOP // 2
NCH = 4096
GROUPS = 32
LANES = 128
RING = 16
PARTS = 17
CHUNKS = 4
ROWS = 32 // CHUNKS
HALF = GROUPS // 2
TALL = WIN // LANES
TIMES = TALL // 2
PER_CHUNK = 8 // CHUNKS
MESH_ID = pl.DeviceIdType.MESH


def split_bf16(table):
    high = table.astype(np.float32).astype(ml_dtypes.bfloat16)
    low = (table - high.astype(np.float64)).astype(ml_dtypes.bfloat16)
    return np.stack([high, low])


def cas(angle):
    return np.cos(angle) + np.sin(angle)


@functools.cache
def tables():
    point = np.arange(LANES)
    blocks = []
    for p in range(TIMES):
        freq = p + TALL * point
        angle = 2.0 * np.pi / WIN * (np.outer(freq, point) % WIN)
        cosine, sine = np.cos(angle), np.sin(angle)
        if p == 0:
            middle = 2.0 * np.pi / WIN * (np.outer(TIMES + freq, point) % WIN)
            none = np.zeros_like(angle)
            blocks.append(np.block([[cas(angle), none], [none, cas(middle)]]))
        else:
            blocks.append(np.block([[cosine, sine], [-sine, cosine]]))
    blocks = np.stack(blocks)
    time = np.stack([split_bf16(blocks), split_bf16(blocks.transpose(0, 2, 1))])
    time = time.transpose(0, 2, 1, 3, 4).reshape(2, TIMES, 4 * LANES, 2 * LANES)
    taper = np.sin(np.pi / WIN * np.arange(WIN)) ** 2
    taper = np.repeat(taper[:, None], LANES, axis=1).astype(np.float32)
    lane = np.arange(LANES)
    angle = 2.0 * np.pi / LANES * (np.outer(lane, lane) % LANES)
    cosine, sine = np.cos(angle), np.sin(angle)
    forward = np.block([[cosine, -sine], [sine, cosine]])
    inverse = np.block([[cosine, sine], [-sine, cosine]])
    chan = np.concatenate([split_bf16(forward), split_bf16(inverse)])
    angle = 2.0 * np.pi / NCH * np.outer(np.arange(PARTS), lane)
    twist = np.stack([np.cos(angle), np.sin(angle)]).astype(np.float32)
    twist = np.repeat(twist[:, :, None, :], 8, axis=2)
    return time, taper, chan, twist


def real_dft(x):
    n = len(x)
    if n == 1:
        return [(x[0], None)]
    if n == 2:
        return [(x[0] + x[1], None), (x[0] - x[1], None)]
    even = real_dft(x[0::2])
    odd = real_dft(x[1::2])
    half = n // 2
    out = [None] * (half + 1)
    out[0] = (even[0][0] + odd[0][0], None)
    out[half] = (even[0][0] - odd[0][0], None)
    for k in range(1, half // 2 + 1):
        e_re, e_im = even[k]
        o_re, o_im = odd[k]
        if 2 * k == half:
            out[k] = (e_re, -o_re)
            continue
        c, s = math.cos(2.0 * math.pi * k / n), math.sin(2.0 * math.pi * k / n)
        t_re = c * o_re + s * o_im
        t_im = c * o_im - s * o_re
        out[k] = (e_re + t_re, e_im + t_im)
        out[half - k] = (e_re - t_re, t_im - e_im)
    return out


def real_inverse(spec):
    half = len(spec) - 1
    n = 2 * half
    first, last = spec[0][0], spec[half][0]
    if n == 2:
        return [first + last, first - last]
    even = [None] * (half // 2 + 1)
    odd = [None] * (half // 2 + 1)
    even[0] = (first + last, None)
    odd[0] = (first - last, None)
    for k in range(1, half // 2 + 1):
        a_re, a_im = spec[k]
        if 2 * k == half:
            even[k] = (2.0 * a_re, None)
            odd[k] = (-2.0 * a_im, None)
            continue
        b_re, b_im = spec[half - k]
        even[k] = (a_re + b_re, a_im - b_im)
        d_re, d_im = a_re - b_re, a_im + b_im
        c, s = math.cos(2.0 * math.pi * k / n), math.sin(2.0 * math.pi * k / n)
        odd[k] = (c * d_re - s * d_im, c * d_im + s * d_re)
    y_even = real_inverse(even)
    y_odd = real_inverse(odd)
    out = []
    for a, b in zip(y_even, y_odd):
        out += [a, b]
    return out


def dot(a, b):
    return jnp.dot(a, b, preferred_element_type=jnp.float32)


def halves(x):
    high = x.astype(jnp.bfloat16)
    low = (x - high.astype(jnp.float32)).astype(jnp.bfloat16)
    return high, low


def table_product(x, high_table, low_table):
    high, low = halves(x)
    return dot(high, high_table) + dot(high, low_table) + dot(low, high_table)


def div(a, b):
    return lax.div(a, jnp.int32(b))


def rem(a, b):
    return lax.rem(a, jnp.int32(b))


def body(
    record_hbm, cuts_hbm, time_hbm, taper_hbm, chan_hbm, twist_hbm,
    out,
    cuts, time, taper, chan, twist,
    stage, recv, spec, coef, block, below, above, limit, lines_time,
    own, spill_low, spill_high, low_in, high_in, arrived, turned, stage_back,
    load_sem, cut_send, cut_sem,
    rows_send, rows_recv, ring_send, ring_recv, wave_send, wave_recv, halo_send, halo_recv,
    spill_send, spill_recv, lines_send, lines_recv, home_send, home_recv, last_send, last_recv,
):
    tm = lax.axis_index("tm")
    chan_index = lax.axis_index("chan")
    zed, side = div(chan_index, 2), rem(chan_index, 2)
    place = 2 * tm + side

    def in_plane(other):
        return {"tm": div(other, 2), "chan": 2 * zed + rem(other, 2)}

    def in_ring(other):
        return {"chan": 2 * other + side}

    up = rem(zed + 1, RING)
    down = rem(zed + RING - 1, RING)

    loads = [pltpu.make_async_copy(taper_hbm, taper, load_sem.at[0])]
    loads += [
        pltpu.make_async_copy(chan_hbm, chan, load_sem.at[1]),
        pltpu.make_async_copy(twist_hbm, twist, load_sem.at[2]),
        pltpu.make_async_copy(time_hbm, time, load_sem.at[3]),
    ]

    def piece(other, chunk):
        return record_hbm.at[pl.ds(pl.multiple_of(32 * other + ROWS * chunk, ROWS), ROWS)]

    mine = [
        pltpu.make_async_copy(piece(place, c), stage.at[c, place], load_sem.at[4 + c])
        for c in range(CHUNKS)
    ]

    barrier = pltpu.get_barrier_semaphore()

    @pl.loop(1, GROUPS)
    def _(step):
        other = rem(place + 11 * step, GROUPS)
        pl.semaphore_signal(barrier, inc=1, device_id=in_plane(other), device_id_type=MESH_ID)

    @pl.loop(1, RING)
    def _(step):
        other = rem(zed + 7 * step, RING)
        pl.semaphore_signal(barrier, inc=1, device_id=in_ring(other), device_id_type=MESH_ID)

    for load in mine + loads:
        load.start()

    pl.semaphore_wait(barrier, GROUPS + RING - 2)

    def remote(source, target, send_sem, recv_sem, device):
        return pltpu.make_async_remote_copy(
            src_ref=source, dst_ref=target, send_sem=send_sem, recv_sem=recv_sem,
            device_id=device, device_id_type=MESH_ID,
        )

    def plane_exchange(source_of, target, send_sem, recv_sem):
        @pl.loop(1, GROUPS)
        def _(step):
            other = rem(place + 11 * step, GROUPS)
            remote(source_of(other), target, send_sem, recv_sem, in_plane(other)).start()

    def ring_exchange(source, target, chunk, send_sem, recv_sem):
        @pl.loop(1, RING)
        def _(step):
            other = rem(zed + 7 * step, RING)
            remote(
                source.at[chunk, pl.ds(2 * other, 2)], target.at[chunk, pl.ds(2 * zed, 2)],
                send_sem.at[chunk], recv_sem.at[chunk], in_ring(other),
            ).start()

        for i in range(2):
            target[chunk, 2 * zed + i] = source[chunk, 2 * zed + i]

    def bytes_of(buffer, count, sem):
        span = buffer.at[0, pl.ds(0, count)]
        return pltpu.make_async_copy(span, span, sem)

    def plane_wait(sem):
        bytes_of(recv, GROUPS - 1, sem).wait()

    def ring_wait(sem):
        bytes_of(recv, GROUPS - 2, sem).wait()

    def send_rows(c):
        plane_exchange(
            lambda other: piece(other, c), stage.at[c, place], rows_send.at[c], rows_recv.at[c]
        )

    send_rows(0)

    @pl.when(tm == zed)
    def _():
        @pl.loop(1, RING)
        def _(step):
            other = rem(tm + step, RING)
            remote(cuts_hbm, cuts, cut_send.at[step], cut_sem.at[0], {"tm": other}).start()

        copy = pltpu.make_async_copy(cuts_hbm, cuts, cut_sem.at[1])
        copy.start()
        copy.wait()

    for c in range(CHUNKS):
        if c + 1 < CHUNKS:
            send_rows(c + 1)
        mine[c].wait()
        plane_wait(rows_recv.at[c])
        ring_exchange(stage, recv, c, ring_send, ring_recv)

    @pl.when(tm != zed)
    def _():
        remote(cuts_hbm, cuts, cut_send.at[0], cut_sem.at[0], {"tm": zed}).wait_recv()

    for p in range(TIMES):
        @pl.loop(0, 8)
        def _(j):
            row = 32 * j + lax.broadcasted_iota(jnp.int32, (32, 1), 0)
            if p == 0:
                freq = jnp.where(row < LANES, TALL * row, TALL * (row - LANES) + TIMES)
            else:
                freq = p + TALL * jnp.where(row < LANES, row, row - LANES)
            band = jnp.minimum(jnp.minimum(freq, WIN - freq), HOP - 1)
            total = jnp.zeros((32, LANES), jnp.int32)
            for i in range(HOP // LANES):
                here = i * LANES + lax.broadcasted_iota(jnp.int32, (32, LANES), 1)
                total = total + jnp.where(here == band, cuts[0:1, i * LANES : (i + 1) * LANES], 0)
            total = jnp.sum(total, axis=1, keepdims=True)
            rows = pl.ds(pl.multiple_of(j * 32, 32), 32)
            limit[p, rows] = jnp.broadcast_to(total, (32, LANES))

    for load in loads:
        load.wait()

    whole = 2 * LANES
    keep_low = jnp.where(zed > 0, 1.0, 0.0).astype(jnp.float32)
    keep_high = jnp.where(zed < RING - 1, 1.0, 0.0).astype(jnp.float32)

    halos = []

    def start_halo(c):
        plane_wait(wave_recv.at[c])
        halos.extend([
            remote(
                block.at[c, pl.ds(HALF, HALF)], below.at[c],
                halo_send.at[2 * c], halo_recv.at[2 * c], in_ring(up),
            ),
            remote(
                block.at[c, pl.ds(0, HALF)], above.at[c],
                halo_send.at[2 * c + 1], halo_recv.at[2 * c + 1], in_ring(down),
            ),
        ])
        for halo in halos[-2:]:
            halo.start()

    quarter = TALL // 4

    def fold(c):
        for halo in halos[2 * c : 2 * c + 2]:
            halo.wait_recv()

        @pl.loop(0, 4)
        def _(a):
            start = 32 * a + ROWS * c
            cells = []
            for i in range(TALL):
                weight = taper[pl.ds(pl.multiple_of(LANES * i + start, 8), ROWS)]
                if i < quarter:
                    cells.append(below[c, 4 * i + a] * (weight * keep_low))
                elif i < 3 * quarter:
                    cells.append(block[c, 4 * (i - quarter) + a] * weight)
                else:
                    cells.append(above[c, 4 * (i - 3 * quarter) + a] * (weight * keep_high))
            here = pl.ds(pl.multiple_of(start, 8), ROWS)
            there = pl.ds(pl.multiple_of(LANES + start, 8), ROWS)
            for p, (re, im) in enumerate(real_dft(cells)):
                if p == TIMES:
                    lines_time[0, there] = re
                else:
                    lines_time[p, here] = re
                    if p > 0:
                        lines_time[p, there] = im

    for c in range(CHUNKS):
        ring_wait(ring_recv.at[c])

        @pl.loop(0, ROWS // 8)
        def _(i):
            rows = pl.ds(pl.multiple_of(i * 8, 8), 8)
            lines = real_dft([recv[c, d, rows] for d in range(GROUPS)])
            for p, (re, im) in enumerate(lines):
                if p == 0:
                    spec[p, rows, 0:LANES] = re
                    spec[p, rows, LANES:whole] = jnp.zeros_like(re)
                elif im is None:
                    spec[p, rows, 0:LANES] = re * twist[0, p]
                    spec[p, rows, LANES:whole] = -(re * twist[1, p])
                else:
                    cosine, sine = twist[0, p], twist[1, p]
                    spec[p, rows, 0:LANES] = re * cosine + im * sine
                    spec[p, rows, LANES:whole] = im * cosine - re * sine

        lines = spec[...].reshape(PARTS * ROWS, whole)
        lines = table_product(lines, chan[0], chan[1]).reshape(PARTS, ROWS, whole)
        for p in range(PARTS):
            re, im = lines[p, :, 0:LANES], lines[p, :, LANES:whole]
            if p == 0:
                coef[c, 0] = re - im
            elif p == PARTS - 1:
                coef[c, GROUPS - 1] = re - im
            else:
                coef[c, 2 * p - 1] = re
                coef[c, 2 * p] = im

        plane_exchange(
            lambda other: coef.at[c, other], block.at[c, place], wave_send.at[c], wave_recv.at[c]
        )
        block[c, place] = coef[c, place]
        if c > 0:
            start_halo(c - 1)
        if c > 1:
            fold(c - 2)

    start_halo(CHUNKS - 1)
    fold(CHUNKS - 2)
    fold(CHUNKS - 1)

    lane = lax.broadcasted_iota(jnp.int32, (1, LANES), 1)
    wave = div(place + 1, 2) + GROUPS * lane
    wave = jnp.minimum(wave, NCH - wave)

    def time_product(way, p, values):
        high, low = halves(values)
        wide = dot(time[way, p], jnp.concatenate([high, low], axis=1))
        main, rest = wide[0:whole], wide[whole : 2 * whole]
        return (main[:, LANES:whole] + rest[:, 0:LANES]) + (rest[:, LANES:whole] + main[:, 0:LANES])

    for p in range(TIMES):
        values = time_product(0, p, lines_time[p])
        lines_time[p] = time_product(1, p, jnp.where(wave <= limit[p], values, 0.0))

    per = LANES // ROWS

    @pl.loop(0, per)
    def _(g):
        here = pl.ds(pl.multiple_of(ROWS * g, ROWS), ROWS)
        there = pl.ds(pl.multiple_of(LANES + ROWS * g, ROWS), ROWS)
        lines = [(lines_time[0, here], None)]
        for p in range(1, TIMES):
            lines.append((lines_time[p, here], lines_time[p, there]))
        lines.append((lines_time[0, there], None))
        for i, value in enumerate(real_inverse(lines)):
            weight = taper[pl.ds(pl.multiple_of(LANES * i + ROWS * g, ROWS), ROWS)]
            value = value * weight
            if i < quarter:
                target, k = spill_low, i
            elif i < 3 * quarter:
                target, k = own, i - quarter
            else:
                target, k = spill_high, i - 3 * quarter
            target[k // PER_CHUNK, per * (k % PER_CHUNK) + g] = value

    spills = {}
    order = [c for pair in zip(range(CHUNKS // 2), range(CHUNKS // 2, CHUNKS)) for c in pair]
    for c in order:
        k = c % (CHUNKS // 2)
        if c < CHUNKS // 2:
            source, target, other = spill_high.at[k], high_in.at[k], up
        else:
            source, target, other = spill_low.at[k], low_in.at[k], down
        spills[c] = remote(source, target, spill_send.at[c], spill_recv.at[c], in_ring(other))
        spills[c].start()

    def send_lines(c):
        spills[c].wait_recv()
        extra, keep = (high_in, keep_low) if c < CHUNKS // 2 else (low_in, keep_high)

        @pl.loop(0, GROUPS)
        def _(q):
            own[c, q] = own[c, q] + extra[c % (CHUNKS // 2), q] * keep

        plane_exchange(
            lambda other: own.at[c, other], arrived.at[c, place], lines_send.at[c], lines_recv.at[c]
        )
        arrived[c, place] = own[c, place]

    send_lines(order[0])
    for step, c in enumerate(order):
        if step + 1 < CHUNKS:
            send_lines(order[step + 1])
        plane_wait(lines_recv.at[c])
        for p in range(PARTS):
            if p == 0 or p == PARTS - 1:
                re = arrived[c, 0 if p == 0 else GROUPS - 1]
                im = -re
            else:
                re, im = arrived[c, 2 * p - 1], arrived[c, 2 * p]
            spec[p, :, 0:LANES] = re
            spec[p, :, LANES:whole] = im
        lines = spec[...].reshape(PARTS * ROWS, whole)
        spec[...] = table_product(lines, chan[2], chan[3]).reshape(PARTS, ROWS, whole)

        @pl.loop(0, ROWS // 8)
        def _(i):
            rows = pl.ds(pl.multiple_of(i * 8, 8), 8)
            lines = []
            for p in range(PARTS):
                re, im = spec[p, rows, 0:LANES], spec[p, rows, LANES:whole]
                cosine, sine = twist[0, p], twist[1, p]
                if p == 0:
                    lines.append((re, None))
                elif p == PARTS - 1:
                    lines.append((re * cosine - im * sine, None))
                else:
                    lines.append((re * cosine - im * sine, im * cosine + re * sine))
            for d, value in enumerate(real_inverse(lines)):
                turned[c, d, rows] = value

        ring_exchange(turned, stage_back, c, home_send, home_recv)

    def final(c):
        return pl.ds(pl.multiple_of(HOP // CHUNKS * c + ROWS * place, ROWS), ROWS)

    for c in order:
        ring_wait(home_recv.at[c])
        plane_exchange(
            lambda other: stage_back.at[c, other], out.at[final(c)], last_send.at[c], last_recv.at[c]
        )
        out[final(c)] = stage_back[c, place]

    for c in range(CHUNKS):
        plane_wait(last_recv.at[c])
    for c in range(CHUNKS):
        for sem in (rows_send, wave_send, lines_send, last_send):
            plane_wait(sem.at[c])
        for sem in (ring_send, home_send):
            ring_wait(sem.at[c])
    for copy in halos + list(spills.values()):
        copy.wait_send()

    @pl.when(tm == zed)
    def _():
        @pl.loop(1, RING)
        def _(step):
            other = rem(tm + step, RING)
            remote(cuts_hbm, cuts, cut_send.at[step], cut_sem.at[0], {"tm": other}).wait_send()


def per_device(record, cuts):
    time, taper, chan, twist = tables()
    blocks = pltpu.VMEM((CHUNKS, GROUPS, ROWS, LANES), jnp.float32)
    half = pltpu.VMEM((CHUNKS, HALF, ROWS, LANES), jnp.float32)
    rim = pltpu.VMEM((CHUNKS // 2, GROUPS, ROWS, LANES), jnp.float32)
    dma = pltpu.SemaphoreType.DMA
    result = pl.pallas_call(
        body,
        out_shape=jax.ShapeDtypeStruct(record.shape, jnp.float32),
        in_specs=[pl.BlockSpec(memory_space=pltpu.HBM)] * 6,
        out_specs=pl.BlockSpec(memory_space=pltpu.VMEM),
        scratch_shapes=[
            pltpu.VMEM(cuts.shape, jnp.int32),
            pltpu.VMEM(time.shape, jnp.bfloat16),
            pltpu.VMEM(taper.shape, jnp.float32),
            pltpu.VMEM(chan.shape, jnp.bfloat16),
            pltpu.VMEM(twist.shape, jnp.float32),
            blocks, blocks,
            pltpu.VMEM((PARTS, ROWS, 2 * LANES), jnp.float32),
            blocks, blocks, half, half,
            pltpu.VMEM((TIMES, 2 * LANES, LANES), jnp.int32),
            pltpu.VMEM((TIMES, 2 * LANES, LANES), jnp.float32),
            blocks, rim, rim, rim, rim, blocks, blocks, blocks,
            dma((4 + CHUNKS,)), dma((RING,)), dma((2,)),
            *[dma((CHUNKS,))] * 6, *[dma((2 * CHUNKS,))] * 2, *[dma((CHUNKS,))] * 8,
        ],
        compiler_params=pltpu.CompilerParams(
            collective_id=0, has_side_effects=True, vmem_limit_bytes=60 * 1024 * 1024
        ),
    )(record, cuts, time, taper, chan, twist)
    return result * (1.0 / (WIN * NCH))


def solution(mesh):
    return jax.shard_map(
        per_device,
        mesh=mesh,
        in_specs=(P("tm", "chan"), P("tm", None)),
        out_specs=P("tm", "chan"),
        check_vma=False,
    )
```

```python
import functools
import math

import jax
import jax.numpy as jnp
import ml_dtypes
import numpy as np
from jax import lax
from jax.experimental import pallas as pl
from jax.experimental.pallas import tpu as pltpu
from jax.sharding import PartitionSpec as P

WIN = 2048
HOP = WIN // 2
RIM = HOP // 2
NCH = 4096
GROUPS = 32
LANES = 128
RING = 16
PARTS = 17
CHUNKS = 4
ROWS = 32 // CHUNKS
HALF = GROUPS // 2
TALL = WIN // LANES
TIMES = TALL // 2
PER_CHUNK = 8 // CHUNKS
MESH_ID = pl.DeviceIdType.MESH


def split_bf16(table):
    high = table.astype(np.float32).astype(ml_dtypes.bfloat16)
    low = (table - high.astype(np.float64)).astype(ml_dtypes.bfloat16)
    return np.stack([high, low])


def cas(angle):
    return np.cos(angle) + np.sin(angle)


@functools.cache
def tables():
    point = np.arange(LANES)
    blocks = []
    for p in range(TIMES):
        freq = p + TALL * point
        angle = 2.0 * np.pi / WIN * (np.outer(freq, point) % WIN)
        cosine, sine = np.cos(angle), np.sin(angle)
        if p == 0:
            middle = 2.0 * np.pi / WIN * (np.outer(TIMES + freq, point) % WIN)
            none = np.zeros_like(angle)
            blocks.append(np.block([[cas(angle), none], [none, cas(middle)]]))
        else:
            blocks.append(np.block([[cosine, sine], [-sine, cosine]]))
    blocks = np.stack(blocks)
    time = np.stack([split_bf16(blocks), split_bf16(blocks.transpose(0, 2, 1))])
    time = time.transpose(0, 2, 1, 3, 4).reshape(2, TIMES, 4 * LANES, 2 * LANES)
    taper = np.sin(np.pi / WIN * np.arange(WIN)) ** 2
    taper = np.repeat(taper[:, None], LANES, axis=1).astype(np.float32)
    lane = np.arange(LANES)
    angle = 2.0 * np.pi / LANES * (np.outer(lane, lane) % LANES)
    cosine, sine = np.cos(angle), np.sin(angle)
    forward = np.block([[cosine, -sine], [sine, cosine]])
    inverse = np.block([[cosine, sine], [-sine, cosine]])
    chan = np.concatenate([split_bf16(forward), split_bf16(inverse)])
    angle = 2.0 * np.pi / NCH * np.outer(np.arange(PARTS), lane)
    twist = np.stack([np.cos(angle), np.sin(angle)]).astype(np.float32)
    twist = np.repeat(twist[:, :, None, :], 8, axis=2)
    return time, taper, chan, twist


def real_dft(x):
    n = len(x)
    if n == 1:
        return [(x[0], None)]
    if n == 2:
        return [(x[0] + x[1], None), (x[0] - x[1], None)]
    even = real_dft(x[0::2])
    odd = real_dft(x[1::2])
    half = n // 2
    out = [None] * (half + 1)
    out[0] = (even[0][0] + odd[0][0], None)
    out[half] = (even[0][0] - odd[0][0], None)
    for k in range(1, half // 2 + 1):
        e_re, e_im = even[k]
        o_re, o_im = odd[k]
        if 2 * k == half:
            out[k] = (e_re, -o_re)
            continue
        c, s = math.cos(2.0 * math.pi * k / n), math.sin(2.0 * math.pi * k / n)
        t_re = c * o_re + s * o_im
        t_im = c * o_im - s * o_re
        out[k] = (e_re + t_re, e_im + t_im)
        out[half - k] = (e_re - t_re, t_im - e_im)
    return out


def real_inverse(spec):
    half = len(spec) - 1
    n = 2 * half
    first, last = spec[0][0], spec[half][0]
    if n == 2:
        return [first + last, first - last]
    even = [None] * (half // 2 + 1)
    odd = [None] * (half // 2 + 1)
    even[0] = (first + last, None)
    odd[0] = (first - last, None)
    for k in range(1, half // 2 + 1):
        a_re, a_im = spec[k]
        if 2 * k == half:
            even[k] = (2.0 * a_re, None)
            odd[k] = (-2.0 * a_im, None)
            continue
        b_re, b_im = spec[half - k]
        even[k] = (a_re + b_re, a_im - b_im)
        d_re, d_im = a_re - b_re, a_im + b_im
        c, s = math.cos(2.0 * math.pi * k / n), math.sin(2.0 * math.pi * k / n)
        odd[k] = (c * d_re - s * d_im, c * d_im + s * d_re)
    y_even = real_inverse(even)
    y_odd = real_inverse(odd)
    out = []
    for a, b in zip(y_even, y_odd):
        out += [a, b]
    return out


def dot(a, b):
    return jnp.dot(a, b, preferred_element_type=jnp.float32)


def halves(x):
    high = x.astype(jnp.bfloat16)
    low = (x - high.astype(jnp.float32)).astype(jnp.bfloat16)
    return high, low


def table_product(x, high_table, low_table):
    high, low = halves(x)
    return dot(high, high_table) + dot(high, low_table) + dot(low, high_table)


def div(a, b):
    return lax.div(a, jnp.int32(b))


def rem(a, b):
    return lax.rem(a, jnp.int32(b))


def body(
    record_hbm, cuts_hbm, time_hbm, taper_hbm, chan_hbm, twist_hbm,
    out,
    cuts, time, taper, chan, twist,
    stage, recv, spec, coef, block, below, above, limit, lines_time,
    own, spill_low, spill_high, low_in, high_in, arrived, turned, stage_back,
    load_sem, cut_send, cut_sem,
    rows_send, rows_recv, ring_send, ring_recv, wave_send, wave_recv, halo_send, halo_recv,
    spill_send, spill_recv, lines_send, lines_recv, home_send, home_recv, last_send, last_recv,
):
    tm = lax.axis_index("tm")
    chan_index = lax.axis_index("chan")
    zed, side = div(chan_index, 2), rem(chan_index, 2)
    place = 2 * tm + side

    def in_plane(other):
        return {"tm": div(other, 2), "chan": 2 * zed + rem(other, 2)}

    def in_ring(other):
        return {"chan": 2 * other + side}

    up = rem(zed + 1, RING)
    down = rem(zed + RING - 1, RING)

    loads = [pltpu.make_async_copy(taper_hbm, taper, load_sem.at[0])]
    loads += [
        pltpu.make_async_copy(chan_hbm, chan, load_sem.at[1]),
        pltpu.make_async_copy(twist_hbm, twist, load_sem.at[2]),
        pltpu.make_async_copy(time_hbm, time, load_sem.at[3]),
    ]

    def piece(other, chunk):
        return record_hbm.at[pl.ds(pl.multiple_of(32 * other + ROWS * chunk, ROWS), ROWS)]

    mine = [
        pltpu.make_async_copy(piece(place, c), stage.at[c, place], load_sem.at[4 + c])
        for c in range(CHUNKS)
    ]

    barrier = pltpu.get_barrier_semaphore()

    for step in range(1, GROUPS):
        other = rem(place + 11 * step % GROUPS, GROUPS)
        pl.semaphore_signal(barrier, inc=1, device_id=in_plane(other), device_id_type=MESH_ID)

    for step in range(1, RING):
        other = rem(zed + 7 * step % RING, RING)
        pl.semaphore_signal(barrier, inc=1, device_id=in_ring(other), device_id_type=MESH_ID)

    for load in mine + loads:
        load.start()

    pl.semaphore_wait(barrier, GROUPS + RING - 2)

    def remote(source, target, send_sem, recv_sem, device):
        return pltpu.make_async_remote_copy(
            src_ref=source, dst_ref=target, send_sem=send_sem, recv_sem=recv_sem,
            device_id=device, device_id_type=MESH_ID,
        )

    def plane_exchange(source_of, target, send_sem, recv_sem):
        for step in range(1, GROUPS):
            other = rem(place + 11 * step % GROUPS, GROUPS)
            remote(source_of(other), target, send_sem, recv_sem, in_plane(other)).start()

    def ring_exchange(source, target, chunk, send_sem, recv_sem):
        for step in range(1, RING):
            other = rem(zed + 7 * step % RING, RING)
            remote(
                source.at[chunk, pl.ds(2 * other, 2)], target.at[chunk, pl.ds(2 * zed, 2)],
                send_sem.at[chunk], recv_sem.at[chunk], in_ring(other),
            ).start()

        for i in range(2):
            target[chunk, 2 * zed + i] = source[chunk, 2 * zed + i]

    def bytes_of(buffer, count, sem):
        span = buffer.at[0, pl.ds(0, count)]
        return pltpu.make_async_copy(span, span, sem)

    def plane_wait(sem):
        bytes_of(recv, GROUPS - 1, sem).wait()

    def ring_wait(sem):
        bytes_of(recv, GROUPS - 2, sem).wait()

    def send_rows(c):
        plane_exchange(
            lambda other: piece(other, c), stage.at[c, place], rows_send.at[c], rows_recv.at[c]
        )

    send_rows(0)

    @pl.when(tm == zed)
    def _():
        @pl.loop(1, RING)
        def _(step):
            other = rem(tm + step, RING)
            remote(cuts_hbm, cuts, cut_send.at[step], cut_sem.at[0], {"tm": other}).start()

        copy = pltpu.make_async_copy(cuts_hbm, cuts, cut_sem.at[1])
        copy.start()
        copy.wait()

    for c in range(CHUNKS):
        if c + 1 < CHUNKS:
            send_rows(c + 1)
        mine[c].wait()
        plane_wait(rows_recv.at[c])
        ring_exchange(stage, recv, c, ring_send, ring_recv)

    @pl.when(tm != zed)
    def _():
        remote(cuts_hbm, cuts, cut_send.at[0], cut_sem.at[0], {"tm": zed}).wait_recv()

    for p in range(TIMES):
        @pl.loop(0, 8)
        def _(j):
            row = 32 * j + lax.broadcasted_iota(jnp.int32, (32, 1), 0)
            if p == 0:
                freq = jnp.where(row < LANES, TALL * row, TALL * (row - LANES) + TIMES)
            else:
                freq = p + TALL * jnp.where(row < LANES, row, row - LANES)
            band = jnp.minimum(jnp.minimum(freq, WIN - freq), HOP - 1)
            total = jnp.zeros((32, LANES), jnp.int32)
            for i in range(HOP // LANES):
                here = i * LANES + lax.broadcasted_iota(jnp.int32, (32, LANES), 1)
                total = total + jnp.where(here == band, cuts[0:1, i * LANES : (i + 1) * LANES], 0)
            total = jnp.sum(total, axis=1, keepdims=True)
            rows = pl.ds(pl.multiple_of(j * 32, 32), 32)
            limit[p, rows] = jnp.broadcast_to(total, (32, LANES))

    for load in loads:
        load.wait()

    whole = 2 * LANES
    keep_low = jnp.where(zed > 0, 1.0, 0.0).astype(jnp.float32)
    keep_high = jnp.where(zed < RING - 1, 1.0, 0.0).astype(jnp.float32)

    halos = []

    def start_halo(c):
        plane_wait(wave_recv.at[c])
        halos.extend([
            remote(
                block.at[c, pl.ds(HALF, HALF)], below.at[c],
                halo_send.at[2 * c], halo_recv.at[2 * c], in_ring(up),
            ),
            remote(
                block.at[c, pl.ds(0, HALF)], above.at[c],
                halo_send.at[2 * c + 1], halo_recv.at[2 * c + 1], in_ring(down),
            ),
        ])
        for halo in halos[-2:]:
            halo.start()

    quarter = TALL // 4

    def fold(c):
        for halo in halos[2 * c : 2 * c + 2]:
            halo.wait_recv()

        @pl.loop(0, 4)
        def _(a):
            start = 32 * a + ROWS * c
            cells = []
            for i in range(TALL):
                weight = taper[pl.ds(pl.multiple_of(LANES * i + start, 8), ROWS)]
                if i < quarter:
                    cells.append(below[c, 4 * i + a] * (weight * keep_low))
                elif i < 3 * quarter:
                    cells.append(block[c, 4 * (i - quarter) + a] * weight)
                else:
                    cells.append(above[c, 4 * (i - 3 * quarter) + a] * (weight * keep_high))
            here = pl.ds(pl.multiple_of(start, 8), ROWS)
            there = pl.ds(pl.multiple_of(LANES + start, 8), ROWS)
            for p, (re, im) in enumerate(real_dft(cells)):
                if p == TIMES:
                    lines_time[0, there] = re
                else:
                    lines_time[p, here] = re
                    if p > 0:
                        lines_time[p, there] = im

    for c in range(CHUNKS):
        ring_wait(ring_recv.at[c])

        @pl.loop(0, ROWS // 8)
        def _(i):
            rows = pl.ds(pl.multiple_of(i * 8, 8), 8)
            lines = real_dft([recv[c, d, rows] for d in range(GROUPS)])
            for p, (re, im) in enumerate(lines):
                if p == 0:
                    spec[p, rows, 0:LANES] = re
                    spec[p, rows, LANES:whole] = jnp.zeros_like(re)
                elif im is None:
                    spec[p, rows, 0:LANES] = re * twist[0, p]
                    spec[p, rows, LANES:whole] = -(re * twist[1, p])
                else:
                    cosine, sine = twist[0, p], twist[1, p]
                    spec[p, rows, 0:LANES] = re * cosine + im * sine
                    spec[p, rows, LANES:whole] = im * cosine - re * sine

        lines = spec[...].reshape(PARTS * ROWS, whole)
        lines = table_product(lines, chan[0], chan[1]).reshape(PARTS, ROWS, whole)
        for p in range(PARTS):
            re, im = lines[p, :, 0:LANES], lines[p, :, LANES:whole]
            if p == 0:
                coef[c, 0] = re - im
            elif p == PARTS - 1:
                coef[c, GROUPS - 1] = re - im
            else:
                coef[c, 2 * p - 1] = re
                coef[c, 2 * p] = im

        plane_exchange(
            lambda other: coef.at[c, other], block.at[c, place], wave_send.at[c], wave_recv.at[c]
        )
        block[c, place] = coef[c, place]
        if c > 0:
            start_halo(c - 1)
        if c > 1:
            fold(c - 2)

    start_halo(CHUNKS - 1)
    fold(CHUNKS - 2)
    fold(CHUNKS - 1)

    lane = lax.broadcasted_iota(jnp.int32, (1, LANES), 1)
    wave = div(place + 1, 2) + GROUPS * lane
    wave = jnp.minimum(wave, NCH - wave)

    def time_product(way, p, values):
        high, low = halves(values)
        wide = dot(time[way, p], jnp.concatenate([high, low], axis=1))
        main, rest = wide[0:whole], wide[whole : 2 * whole]
        return (main[:, LANES:whole] + rest[:, 0:LANES]) + (rest[:, LANES:whole] + main[:, 0:LANES])

    for p in range(TIMES):
        values = time_product(0, p, lines_time[p])
        lines_time[p] = time_product(1, p, jnp.where(wave <= limit[p], values, 0.0))

    per = LANES // ROWS

    @pl.loop(0, per)
    def _(g):
        here = pl.ds(pl.multiple_of(ROWS * g, ROWS), ROWS)
        there = pl.ds(pl.multiple_of(LANES + ROWS * g, ROWS), ROWS)
        lines = [(lines_time[0, here], None)]
        for p in range(1, TIMES):
            lines.append((lines_time[p, here], lines_time[p, there]))
        lines.append((lines_time[0, there], None))
        for i, value in enumerate(real_inverse(lines)):
            weight = taper[pl.ds(pl.multiple_of(LANES * i + ROWS * g, ROWS), ROWS)]
            value = value * weight
            if i < quarter:
                target, k = spill_low, i
            elif i < 3 * quarter:
                target, k = own, i - quarter
            else:
                target, k = spill_high, i - 3 * quarter
            target[k // PER_CHUNK, per * (k % PER_CHUNK) + g] = value

    spills = {}
    order = [c for pair in zip(range(CHUNKS // 2), range(CHUNKS // 2, CHUNKS)) for c in pair]
    for c in order:
        k = c % (CHUNKS // 2)
        if c < CHUNKS // 2:
            source, target, other = spill_high.at[k], high_in.at[k], up
        else:
            source, target, other = spill_low.at[k], low_in.at[k], down
        spills[c] = remote(source, target, spill_send.at[c], spill_recv.at[c], in_ring(other))
        spills[c].start()

    def send_lines(c):
        spills[c].wait_recv()
        extra, keep = (high_in, keep_low) if c < CHUNKS // 2 else (low_in, keep_high)

        @pl.loop(0, GROUPS)
        def _(q):
            own[c, q] = own[c, q] + extra[c % (CHUNKS // 2), q] * keep

        plane_exchange(
            lambda other: own.at[c, other], arrived.at[c, place], lines_send.at[c], lines_recv.at[c]
        )
        arrived[c, place] = own[c, place]

    send_lines(order[0])
    for step, c in enumerate(order):
        if step + 1 < CHUNKS:
            send_lines(order[step + 1])
        plane_wait(lines_recv.at[c])
        for p in range(PARTS):
            if p == 0 or p == PARTS - 1:
                re = arrived[c, 0 if p == 0 else GROUPS - 1]
                im = -re
            else:
                re, im = arrived[c, 2 * p - 1], arrived[c, 2 * p]
            spec[p, :, 0:LANES] = re
            spec[p, :, LANES:whole] = im
        lines = spec[...].reshape(PARTS * ROWS, whole)
        spec[...] = table_product(lines, chan[2], chan[3]).reshape(PARTS, ROWS, whole)

        @pl.loop(0, ROWS // 8)
        def _(i):
            rows = pl.ds(pl.multiple_of(i * 8, 8), 8)
            lines = []
            for p in range(PARTS):
                re, im = spec[p, rows, 0:LANES], spec[p, rows, LANES:whole]
                cosine, sine = twist[0, p], twist[1, p]
                if p == 0:
                    lines.append((re, None))
                elif p == PARTS - 1:
                    lines.append((re * cosine - im * sine, None))
                else:
                    lines.append((re * cosine - im * sine, im * cosine + re * sine))
            for d, value in enumerate(real_inverse(lines)):
                turned[c, d, rows] = value

        ring_exchange(turned, stage_back, c, home_send, home_recv)

    def final(c):
        return pl.ds(pl.multiple_of(HOP // CHUNKS * c + ROWS * place, ROWS), ROWS)

    for c in order:
        ring_wait(home_recv.at[c])
        plane_exchange(
            lambda other: stage_back.at[c, other], out.at[final(c)], last_send.at[c], last_recv.at[c]
        )
        out[final(c)] = stage_back[c, place]

    for c in range(CHUNKS):
        plane_wait(last_recv.at[c])
    for c in range(CHUNKS):
        for sem in (rows_send, wave_send, lines_send, last_send):
            plane_wait(sem.at[c])
        for sem in (ring_send, home_send):
            ring_wait(sem.at[c])
    for copy in halos + list(spills.values()):
        copy.wait_send()

    @pl.when(tm == zed)
    def _():
        @pl.loop(1, RING)
        def _(step):
            other = rem(tm + step, RING)
            remote(cuts_hbm, cuts, cut_send.at[step], cut_sem.at[0], {"tm": other}).wait_send()


def per_device(record, cuts):
    time, taper, chan, twist = tables()
    blocks = pltpu.VMEM((CHUNKS, GROUPS, ROWS, LANES), jnp.float32)
    half = pltpu.VMEM((CHUNKS, HALF, ROWS, LANES), jnp.float32)
    rim = pltpu.VMEM((CHUNKS // 2, GROUPS, ROWS, LANES), jnp.float32)
    dma = pltpu.SemaphoreType.DMA
    result = pl.pallas_call(
        body,
        out_shape=jax.ShapeDtypeStruct(record.shape, jnp.float32),
        in_specs=[pl.BlockSpec(memory_space=pltpu.HBM)] * 6,
        out_specs=pl.BlockSpec(memory_space=pltpu.VMEM),
        scratch_shapes=[
            pltpu.VMEM(cuts.shape, jnp.int32),
            pltpu.VMEM(time.shape, jnp.bfloat16),
            pltpu.VMEM(taper.shape, jnp.float32),
            pltpu.VMEM(chan.shape, jnp.bfloat16),
            pltpu.VMEM(twist.shape, jnp.float32),
            blocks, blocks,
            pltpu.VMEM((PARTS, ROWS, 2 * LANES), jnp.float32),
            blocks, blocks, half, half,
            pltpu.VMEM((TIMES, 2 * LANES, LANES), jnp.int32),
            pltpu.VMEM((TIMES, 2 * LANES, LANES), jnp.float32),
            blocks, rim, rim, rim, rim, blocks, blocks, blocks,
            dma((4 + CHUNKS,)), dma((RING,)), dma((2,)),
            *[dma((CHUNKS,))] * 6, *[dma((2 * CHUNKS,))] * 2, *[dma((CHUNKS,))] * 8,
        ],
        compiler_params=pltpu.CompilerParams(
            collective_id=0, has_side_effects=True, vmem_limit_bytes=60 * 1024 * 1024
        ),
    )(record, cuts, time, taper, chan, twist)
    return result * (1.0 / (WIN * NCH))


def solution(mesh):
    return jax.shard_map(
        per_device,
        mesh=mesh,
        in_specs=(P("tm", "chan"), P("tm", None)),
        out_specs=P("tm", "chan"),
        check_vma=False,
    )
```

```python
import functools
import math

import jax
import jax.numpy as jnp
import ml_dtypes
import numpy as np
from jax import lax
from jax.experimental import pallas as pl
from jax.experimental.pallas import tpu as pltpu
from jax.sharding import PartitionSpec as P

WIN = 2048
HOP = WIN // 2
RIM = HOP // 2
NCH = 4096
GROUPS = 32
LANES = 128
RING = 16
PARTS = 17
CHUNKS = 4
ROWS = 32 // CHUNKS
HALF = GROUPS // 2
TALL = WIN // LANES
TIMES = TALL // 2
PER_CHUNK = 8 // CHUNKS
MESH_ID = pl.DeviceIdType.MESH


def split_bf16(table):
    high = table.astype(np.float32).astype(ml_dtypes.bfloat16)
    low = (table - high.astype(np.float64)).astype(ml_dtypes.bfloat16)
    return np.stack([high, low])


def cas(angle):
    return np.cos(angle) + np.sin(angle)


@functools.cache
def tables():
    point = np.arange(LANES)
    blocks = []
    for p in range(TIMES):
        freq = p + TALL * point
        angle = 2.0 * np.pi / WIN * (np.outer(freq, point) % WIN)
        cosine, sine = np.cos(angle), np.sin(angle)
        if p == 0:
            middle = 2.0 * np.pi / WIN * (np.outer(TIMES + freq, point) % WIN)
            none = np.zeros_like(angle)
            blocks.append(np.block([[cas(angle), none], [none, cas(middle)]]))
        else:
            blocks.append(np.block([[cosine, sine], [-sine, cosine]]))
    blocks = np.stack(blocks)
    time = np.stack([split_bf16(blocks), split_bf16(blocks.transpose(0, 2, 1))])
    time = time.transpose(0, 2, 1, 3, 4).reshape(2, TIMES, 4 * LANES, 2 * LANES)
    taper = np.sin(np.pi / WIN * np.arange(WIN)) ** 2
    taper = np.repeat(taper[:, None], LANES, axis=1).astype(np.float32)
    lane = np.arange(LANES)
    angle = 2.0 * np.pi / LANES * (np.outer(lane, lane) % LANES)
    cosine, sine = np.cos(angle), np.sin(angle)
    forward = np.block([[cosine, -sine], [sine, cosine]])
    inverse = np.block([[cosine, sine], [-sine, cosine]])
    chan = np.concatenate([split_bf16(forward), split_bf16(inverse)])
    angle = 2.0 * np.pi / NCH * np.outer(np.arange(PARTS), lane)
    twist = np.stack([np.cos(angle), np.sin(angle)]).astype(np.float32)
    twist = np.repeat(twist[:, :, None, :], 8, axis=2)
    return time, taper, chan, twist


def real_dft(x):
    n = len(x)
    if n == 1:
        return [(x[0], None)]
    if n == 2:
        return [(x[0] + x[1], None), (x[0] - x[1], None)]
    even = real_dft(x[0::2])
    odd = real_dft(x[1::2])
    half = n // 2
    out = [None] * (half + 1)
    out[0] = (even[0][0] + odd[0][0], None)
    out[half] = (even[0][0] - odd[0][0], None)
    for k in range(1, half // 2 + 1):
        e_re, e_im = even[k]
        o_re, o_im = odd[k]
        if 2 * k == half:
            out[k] = (e_re, -o_re)
            continue
        c, s = math.cos(2.0 * math.pi * k / n), math.sin(2.0 * math.pi * k / n)
        t_re = c * o_re + s * o_im
        t_im = c * o_im - s * o_re
        out[k] = (e_re + t_re, e_im + t_im)
        out[half - k] = (e_re - t_re, t_im - e_im)
    return out


def real_inverse(spec):
    half = len(spec) - 1
    n = 2 * half
    first, last = spec[0][0], spec[half][0]
    if n == 2:
        return [first + last, first - last]
    even = [None] * (half // 2 + 1)
    odd = [None] * (half // 2 + 1)
    even[0] = (first + last, None)
    odd[0] = (first - last, None)
    for k in range(1, half // 2 + 1):
        a_re, a_im = spec[k]
        if 2 * k == half:
            even[k] = (2.0 * a_re, None)
            odd[k] = (-2.0 * a_im, None)
            continue
        b_re, b_im = spec[half - k]
        even[k] = (a_re + b_re, a_im - b_im)
        d_re, d_im = a_re - b_re, a_im + b_im
        c, s = math.cos(2.0 * math.pi * k / n), math.sin(2.0 * math.pi * k / n)
        odd[k] = (c * d_re - s * d_im, c * d_im + s * d_re)
    y_even = real_inverse(even)
    y_odd = real_inverse(odd)
    out = []
    for a, b in zip(y_even, y_odd):
        out += [a, b]
    return out


def dot(a, b):
    return jnp.dot(a, b, preferred_element_type=jnp.float32)


def halves(x):
    high = x.astype(jnp.bfloat16)
    low = (x - high.astype(jnp.float32)).astype(jnp.bfloat16)
    return high, low


def table_product(x, high_table, low_table):
    high, low = halves(x)
    return dot(high, high_table) + dot(high, low_table) + dot(low, high_table)


def div(a, b):
    return lax.div(a, jnp.int32(b))


def rem(a, b):
    return lax.rem(a, jnp.int32(b))


def body(
    record_hbm, cuts_hbm, time_hbm, taper_hbm, chan_hbm, twist_hbm,
    out,
    cuts, time, taper, chan, twist,
    stage, recv, spec, coef, block, below, above, limit, lines_time,
    own, spill_low, spill_high, low_in, high_in, arrived, turned, stage_back,
    load_sem, cut_send, cut_sem,
    rows_send, rows_recv, ring_send, ring_recv, wave_send, wave_recv, halo_send, halo_recv,
    spill_send, spill_recv, lines_send, lines_recv, home_send, home_recv, last_send, last_recv,
):
    tm = lax.axis_index("tm")
    chan_index = lax.axis_index("chan")
    zed, side = div(chan_index, 2), rem(chan_index, 2)
    place = 2 * tm + side

    def in_plane(other):
        return {"tm": div(other, 2), "chan": 2 * zed + rem(other, 2)}

    def in_ring(other):
        return {"chan": 2 * other + side}

    up = rem(zed + 1, RING)
    down = rem(zed + RING - 1, RING)

    loads = [pltpu.make_async_copy(taper_hbm, taper, load_sem.at[0])]
    loads += [
        pltpu.make_async_copy(chan_hbm, chan, load_sem.at[1]),
        pltpu.make_async_copy(twist_hbm, twist, load_sem.at[2]),
        pltpu.make_async_copy(time_hbm, time, load_sem.at[3]),
    ]

    def piece(other, chunk):
        return record_hbm.at[pl.ds(pl.multiple_of(32 * other + ROWS * chunk, ROWS), ROWS)]

    mine = [
        pltpu.make_async_copy(piece(place, c), stage.at[c, place], load_sem.at[4 + c])
        for c in range(CHUNKS)
    ]

    barrier = pltpu.get_barrier_semaphore()

    for step in range(1, GROUPS):
        other = rem(place + 11 * step % GROUPS, GROUPS)
        pl.semaphore_signal(barrier, inc=1, device_id=in_plane(other), device_id_type=MESH_ID)

    for step in range(1, RING):
        other = rem(zed + 7 * step % RING, RING)
        pl.semaphore_signal(barrier, inc=1, device_id=in_ring(other), device_id_type=MESH_ID)

    for load in mine + loads:
        load.start()

    pl.semaphore_wait(barrier, GROUPS + RING - 2)

    def remote(source, target, send_sem, recv_sem, device):
        return pltpu.make_async_remote_copy(
            src_ref=source, dst_ref=target, send_sem=send_sem, recv_sem=recv_sem,
            device_id=device, device_id_type=MESH_ID,
        )

    def plane_exchange(source_of, target, send_sem, recv_sem):
        for step in range(1, GROUPS):
            other = rem(place + 11 * step % GROUPS, GROUPS)
            remote(source_of(other), target, send_sem, recv_sem, in_plane(other)).start()

    def ring_exchange(source, target, chunk, send_sem, recv_sem):
        for step in range(1, RING):
            other = rem(zed + 7 * step % RING, RING)
            remote(
                source.at[chunk, pl.ds(2 * other, 2)], target.at[chunk, pl.ds(2 * zed, 2)],
                send_sem.at[chunk], recv_sem.at[chunk], in_ring(other),
            ).start()

        for i in range(2):
            target[chunk, 2 * zed + i] = source[chunk, 2 * zed + i]

    def bytes_of(buffer, count, sem):
        span = buffer.at[0, pl.ds(0, count)]
        return pltpu.make_async_copy(span, span, sem)

    def plane_wait(sem):
        bytes_of(recv, GROUPS - 1, sem).wait()

    def ring_wait(sem):
        bytes_of(recv, GROUPS - 2, sem).wait()

    def send_rows(c):
        plane_exchange(
            lambda other: piece(other, c), stage.at[c, place], rows_send.at[c], rows_recv.at[c]
        )

    send_rows(0)

    @pl.when(tm == zed)
    def _():
        @pl.loop(1, RING)
        def _(step):
            other = rem(tm + step, RING)
            remote(cuts_hbm, cuts, cut_send.at[step], cut_sem.at[0], {"tm": other}).start()

        copy = pltpu.make_async_copy(cuts_hbm, cuts, cut_sem.at[1])
        copy.start()
        copy.wait()

    def send_ring(c):
        mine[c].wait()
        plane_wait(rows_recv.at[c])
        if c > 1:
            ring_wait(ring_recv.at[c - 2])
        ring_exchange(stage, recv, c, ring_send, ring_recv)
        if c + 1 < CHUNKS:
            send_rows(c + 1)

    send_ring(0)
    send_ring(1)

    @pl.when(tm != zed)
    def _():
        remote(cuts_hbm, cuts, cut_send.at[0], cut_sem.at[0], {"tm": zed}).wait_recv()

    for p in range(TIMES):
        @pl.loop(0, 8)
        def _(j):
            row = 32 * j + lax.broadcasted_iota(jnp.int32, (32, 1), 0)
            if p == 0:
                freq = jnp.where(row < LANES, TALL * row, TALL * (row - LANES) + TIMES)
            else:
                freq = p + TALL * jnp.where(row < LANES, row, row - LANES)
            band = jnp.minimum(jnp.minimum(freq, WIN - freq), HOP - 1)
            total = jnp.zeros((32, LANES), jnp.int32)
            for i in range(HOP // LANES):
                here = i * LANES + lax.broadcasted_iota(jnp.int32, (32, LANES), 1)
                total = total + jnp.where(here == band, cuts[0:1, i * LANES : (i + 1) * LANES], 0)
            total = jnp.sum(total, axis=1, keepdims=True)
            rows = pl.ds(pl.multiple_of(j * 32, 32), 32)
            limit[p, rows] = jnp.broadcast_to(total, (32, LANES))

    for load in loads:
        load.wait()

    whole = 2 * LANES
    keep_low = jnp.where(zed > 0, 1.0, 0.0).astype(jnp.float32)
    keep_high = jnp.where(zed < RING - 1, 1.0, 0.0).astype(jnp.float32)

    halos = []

    def start_halo(c):
        plane_wait(wave_recv.at[c])
        halos.extend([
            remote(
                block.at[c, pl.ds(HALF, HALF)], below.at[c],
                halo_send.at[2 * c], halo_recv.at[2 * c], in_ring(up),
            ),
            remote(
                block.at[c, pl.ds(0, HALF)], above.at[c],
                halo_send.at[2 * c + 1], halo_recv.at[2 * c + 1], in_ring(down),
            ),
        ])
        for halo in halos[-2:]:
            halo.start()

    quarter = TALL // 4

    def fold(c):
        for halo in halos[2 * c : 2 * c + 2]:
            halo.wait_recv()

        @pl.loop(0, 4)
        def _(a):
            start = 32 * a + ROWS * c
            cells = []
            for i in range(TALL):
                weight = taper[pl.ds(pl.multiple_of(LANES * i + start, 8), ROWS)]
                if i < quarter:
                    cells.append(below[c, 4 * i + a] * (weight * keep_low))
                elif i < 3 * quarter:
                    cells.append(block[c, 4 * (i - quarter) + a] * weight)
                else:
                    cells.append(above[c, 4 * (i - 3 * quarter) + a] * (weight * keep_high))
            here = pl.ds(pl.multiple_of(start, 8), ROWS)
            there = pl.ds(pl.multiple_of(LANES + start, 8), ROWS)
            for p, (re, im) in enumerate(real_dft(cells)):
                if p == TIMES:
                    lines_time[0, there] = re
                else:
                    lines_time[p, here] = re
                    if p > 0:
                        lines_time[p, there] = im

    for c in range(CHUNKS):
        if c + 2 < CHUNKS:
            send_ring(c + 2)
        else:
            ring_wait(ring_recv.at[c])

        @pl.loop(0, ROWS // 8)
        def _(i):
            rows = pl.ds(pl.multiple_of(i * 8, 8), 8)
            lines = real_dft([recv[c, d, rows] for d in range(GROUPS)])
            for p, (re, im) in enumerate(lines):
                if p == 0:
                    spec[p, rows, 0:LANES] = re
                    spec[p, rows, LANES:whole] = jnp.zeros_like(re)
                elif im is None:
                    spec[p, rows, 0:LANES] = re * twist[0, p]
                    spec[p, rows, LANES:whole] = -(re * twist[1, p])
                else:
                    cosine, sine = twist[0, p], twist[1, p]
                    spec[p, rows, 0:LANES] = re * cosine + im * sine
                    spec[p, rows, LANES:whole] = im * cosine - re * sine

        lines = spec[...].reshape(PARTS * ROWS, whole)
        lines = table_product(lines, chan[0], chan[1]).reshape(PARTS, ROWS, whole)
        for p in range(PARTS):
            re, im = lines[p, :, 0:LANES], lines[p, :, LANES:whole]
            if p == 0:
                coef[c, 0] = re - im
            elif p == PARTS - 1:
                coef[c, GROUPS - 1] = re - im
            else:
                coef[c, 2 * p - 1] = re
                coef[c, 2 * p] = im

        plane_exchange(
            lambda other: coef.at[c, other], block.at[c, place], wave_send.at[c], wave_recv.at[c]
        )
        block[c, place] = coef[c, place]
        if c > 0:
            start_halo(c - 1)
        if c > 1:
            fold(c - 2)

    start_halo(CHUNKS - 1)
    fold(CHUNKS - 2)
    fold(CHUNKS - 1)

    lane = lax.broadcasted_iota(jnp.int32, (1, LANES), 1)
    wave = div(place + 1, 2) + GROUPS * lane
    wave = jnp.minimum(wave, NCH - wave)

    def time_product(way, p, values):
        high, low = halves(values)
        wide = dot(time[way, p], jnp.concatenate([high, low], axis=1))
        main, rest = wide[0:whole], wide[whole : 2 * whole]
        return (main[:, LANES:whole] + rest[:, 0:LANES]) + (rest[:, LANES:whole] + main[:, 0:LANES])

    for p in range(TIMES):
        values = time_product(0, p, lines_time[p])
        lines_time[p] = time_product(1, p, jnp.where(wave <= limit[p], values, 0.0))

    per = LANES // ROWS

    @pl.loop(0, per)
    def _(g):
        here = pl.ds(pl.multiple_of(ROWS * g, ROWS), ROWS)
        there = pl.ds(pl.multiple_of(LANES + ROWS * g, ROWS), ROWS)
        lines = [(lines_time[0, here], None)]
        for p in range(1, TIMES):
            lines.append((lines_time[p, here], lines_time[p, there]))
        lines.append((lines_time[0, there], None))
        for i, value in enumerate(real_inverse(lines)):
            weight = taper[pl.ds(pl.multiple_of(LANES * i + ROWS * g, ROWS), ROWS)]
            value = value * weight
            if i < quarter:
                target, k = spill_low, i
            elif i < 3 * quarter:
                target, k = own, i - quarter
            else:
                target, k = spill_high, i - 3 * quarter
            target[k // PER_CHUNK, per * (k % PER_CHUNK) + g] = value

    spills = {}
    order = [c for pair in zip(range(CHUNKS // 2), range(CHUNKS // 2, CHUNKS)) for c in pair]
    for c in order:
        k = c % (CHUNKS // 2)
        if c < CHUNKS // 2:
            source, target, other = spill_high.at[k], high_in.at[k], up
        else:
            source, target, other = spill_low.at[k], low_in.at[k], down
        spills[c] = remote(source, target, spill_send.at[c], spill_recv.at[c], in_ring(other))
    for c in order[:2]:
        spills[c].start()

    def send_lines(c):
        spills[c].wait_recv()
        if c == order[0]:
            for later in order[2:]:
                spills[later].start()
        extra, keep = (high_in, keep_low) if c < CHUNKS // 2 else (low_in, keep_high)

        @pl.loop(0, GROUPS)
        def _(q):
            own[c, q] = own[c, q] + extra[c % (CHUNKS // 2), q] * keep

        plane_exchange(
            lambda other: own.at[c, other], arrived.at[c, place], lines_send.at[c], lines_recv.at[c]
        )
        arrived[c, place] = own[c, place]

    def send_home(c):
        final = pl.ds(pl.multiple_of(HOP // CHUNKS * c + ROWS * place, ROWS), ROWS)
        plane_exchange(
            lambda other: stage_back.at[c, other], out.at[final], last_send.at[c], last_recv.at[c]
        )
        out[final] = stage_back[c, place]

    send_lines(order[0])
    for step, c in enumerate(order):
        plane_wait(lines_recv.at[c])
        if step + 1 < CHUNKS:
            send_lines(order[step + 1])
        for p in range(PARTS):
            if p == 0 or p == PARTS - 1:
                re = arrived[c, 0 if p == 0 else GROUPS - 1]
                im = -re
            else:
                re, im = arrived[c, 2 * p - 1], arrived[c, 2 * p]
            spec[p, :, 0:LANES] = re
            spec[p, :, LANES:whole] = im
        lines = spec[...].reshape(PARTS * ROWS, whole)
        spec[...] = table_product(lines, chan[2], chan[3]).reshape(PARTS, ROWS, whole)

        @pl.loop(0, ROWS // 8)
        def _(i):
            rows = pl.ds(pl.multiple_of(i * 8, 8), 8)
            lines = []
            for p in range(PARTS):
                re, im = spec[p, rows, 0:LANES], spec[p, rows, LANES:whole]
                cosine, sine = twist[0, p], twist[1, p]
                if p == 0:
                    lines.append((re, None))
                elif p == PARTS - 1:
                    lines.append((re * cosine - im * sine, None))
                else:
                    lines.append((re * cosine - im * sine, im * cosine + re * sine))
            for d, value in enumerate(real_inverse(lines)):
                turned[c, d, rows] = value

        if step > 1:
            ring_wait(home_recv.at[order[step - 2]])
        ring_exchange(turned, stage_back, c, home_send, home_recv)
        if step > 1:
            send_home(order[step - 2])

    for c in order[-2:]:
        ring_wait(home_recv.at[c])
        send_home(c)

    for c in range(CHUNKS):
        plane_wait(last_recv.at[c])
    for c in range(CHUNKS):
        for sem in (rows_send, wave_send, lines_send, last_send):
            plane_wait(sem.at[c])
        for sem in (ring_send, home_send):
            ring_wait(sem.at[c])
    for copy in halos + list(spills.values()):
        copy.wait_send()

    @pl.when(tm == zed)
    def _():
        @pl.loop(1, RING)
        def _(step):
            other = rem(tm + step, RING)
            remote(cuts_hbm, cuts, cut_send.at[step], cut_sem.at[0], {"tm": other}).wait_send()


def per_device(record, cuts):
    time, taper, chan, twist = tables()
    blocks = pltpu.VMEM((CHUNKS, GROUPS, ROWS, LANES), jnp.float32)
    half = pltpu.VMEM((CHUNKS, HALF, ROWS, LANES), jnp.float32)
    rim = pltpu.VMEM((CHUNKS // 2, GROUPS, ROWS, LANES), jnp.float32)
    dma = pltpu.SemaphoreType.DMA
    result = pl.pallas_call(
        body,
        out_shape=jax.ShapeDtypeStruct(record.shape, jnp.float32),
        in_specs=[pl.BlockSpec(memory_space=pltpu.HBM)] * 6,
        out_specs=pl.BlockSpec(memory_space=pltpu.VMEM),
        scratch_shapes=[
            pltpu.VMEM(cuts.shape, jnp.int32),
            pltpu.VMEM(time.shape, jnp.bfloat16),
            pltpu.VMEM(taper.shape, jnp.float32),
            pltpu.VMEM(chan.shape, jnp.bfloat16),
            pltpu.VMEM(twist.shape, jnp.float32),
            blocks, blocks,
            pltpu.VMEM((PARTS, ROWS, 2 * LANES), jnp.float32),
            blocks, blocks, half, half,
            pltpu.VMEM((TIMES, 2 * LANES, LANES), jnp.int32),
            pltpu.VMEM((TIMES, 2 * LANES, LANES), jnp.float32),
            blocks, rim, rim, rim, rim, blocks, blocks, blocks,
            dma((4 + CHUNKS,)), dma((RING,)), dma((2,)),
            *[dma((CHUNKS,))] * 6, *[dma((2 * CHUNKS,))] * 2, *[dma((CHUNKS,))] * 8,
        ],
        compiler_params=pltpu.CompilerParams(
            collective_id=0, has_side_effects=True, vmem_limit_bytes=60 * 1024 * 1024
        ),
    )(record, cuts, time, taper, chan, twist)
    return result * (1.0 / (WIN * NCH))


def solution(mesh):
    return jax.shard_map(
        per_device,
        mesh=mesh,
        in_specs=(P("tm", "chan"), P("tm", None)),
        out_specs=P("tm", "chan"),
        check_vma=False,
    )
```

```python
import functools
import math

import jax
import jax.numpy as jnp
import ml_dtypes
import numpy as np
from jax import lax
from jax.experimental import pallas as pl
from jax.experimental.pallas import tpu as pltpu
from jax.sharding import PartitionSpec as P

WIN = 2048
HOP = WIN // 2
RIM = HOP // 2
NCH = 4096
GROUPS = 32
LANES = 128
RING = 16
PARTS = 17
CHUNKS = 4
ROWS = 32 // CHUNKS
HALF = GROUPS // 2
TALL = WIN // LANES
TIMES = TALL // 2
PER_CHUNK = 8 // CHUNKS
MESH_ID = pl.DeviceIdType.MESH


def split_bf16(table):
    high = table.astype(np.float32).astype(ml_dtypes.bfloat16)
    low = (table - high.astype(np.float64)).astype(ml_dtypes.bfloat16)
    return np.stack([high, low])


def cas(angle):
    return np.cos(angle) + np.sin(angle)


@functools.cache
def tables():
    point = np.arange(LANES)
    blocks = []
    for p in range(TIMES):
        freq = p + TALL * point
        angle = 2.0 * np.pi / WIN * (np.outer(freq, point) % WIN)
        cosine, sine = np.cos(angle), np.sin(angle)
        if p == 0:
            middle = 2.0 * np.pi / WIN * (np.outer(TIMES + freq, point) % WIN)
            none = np.zeros_like(angle)
            blocks.append(np.block([[cas(angle), none], [none, cas(middle)]]))
        else:
            blocks.append(np.block([[cosine, sine], [-sine, cosine]]))
    blocks = np.stack(blocks)
    time = np.stack([split_bf16(blocks), split_bf16(blocks.transpose(0, 2, 1))])
    time = time.transpose(0, 2, 1, 3, 4).reshape(2, TIMES, 4 * LANES, 2 * LANES)
    taper = np.sin(np.pi / WIN * np.arange(WIN)) ** 2
    taper = np.repeat(taper[:, None], LANES, axis=1).astype(np.float32)
    lane = np.arange(LANES)
    angle = 2.0 * np.pi / LANES * (np.outer(lane, lane) % LANES)
    cosine, sine = np.cos(angle), np.sin(angle)
    forward = np.block([[cosine, -sine], [sine, cosine]])
    inverse = np.block([[cosine, sine], [-sine, cosine]])
    chan = np.concatenate([split_bf16(forward), split_bf16(inverse)])
    angle = 2.0 * np.pi / NCH * np.outer(np.arange(PARTS), lane)
    twist = np.stack([np.cos(angle), np.sin(angle)]).astype(np.float32)
    twist = np.repeat(twist[:, :, None, :], 8, axis=2)
    return time, taper, chan, twist


def real_dft(x):
    n = len(x)
    if n == 1:
        return [(x[0], None)]
    if n == 2:
        return [(x[0] + x[1], None), (x[0] - x[1], None)]
    even = real_dft(x[0::2])
    odd = real_dft(x[1::2])
    half = n // 2
    out = [None] * (half + 1)
    out[0] = (even[0][0] + odd[0][0], None)
    out[half] = (even[0][0] - odd[0][0], None)
    for k in range(1, half // 2 + 1):
        e_re, e_im = even[k]
        o_re, o_im = odd[k]
        if 2 * k == half:
            out[k] = (e_re, -o_re)
            continue
        c, s = math.cos(2.0 * math.pi * k / n), math.sin(2.0 * math.pi * k / n)
        t_re = c * o_re + s * o_im
        t_im = c * o_im - s * o_re
        out[k] = (e_re + t_re, e_im + t_im)
        out[half - k] = (e_re - t_re, t_im - e_im)
    return out


def real_inverse(spec):
    half = len(spec) - 1
    n = 2 * half
    first, last = spec[0][0], spec[half][0]
    if n == 2:
        return [first + last, first - last]
    even = [None] * (half // 2 + 1)
    odd = [None] * (half // 2 + 1)
    even[0] = (first + last, None)
    odd[0] = (first - last, None)
    for k in range(1, half // 2 + 1):
        a_re, a_im = spec[k]
        if 2 * k == half:
            even[k] = (2.0 * a_re, None)
            odd[k] = (-2.0 * a_im, None)
            continue
        b_re, b_im = spec[half - k]
        even[k] = (a_re + b_re, a_im - b_im)
        d_re, d_im = a_re - b_re, a_im + b_im
        c, s = math.cos(2.0 * math.pi * k / n), math.sin(2.0 * math.pi * k / n)
        odd[k] = (c * d_re - s * d_im, c * d_im + s * d_re)
    y_even = real_inverse(even)
    y_odd = real_inverse(odd)
    out = []
    for a, b in zip(y_even, y_odd):
        out += [a, b]
    return out


def dot(a, b):
    return jnp.dot(a, b, preferred_element_type=jnp.float32)


def halves(x):
    high = x.astype(jnp.bfloat16)
    low = (x - high.astype(jnp.float32)).astype(jnp.bfloat16)
    return high, low


def table_product(x, high_table, low_table):
    high, low = halves(x)
    return dot(high, high_table) + dot(high, low_table) + dot(low, high_table)


def div(a, b):
    return lax.div(a, jnp.int32(b))


def rem(a, b):
    return lax.rem(a, jnp.int32(b))


def body(
    record_hbm, cuts_hbm, time_hbm, taper_hbm, chan_hbm, twist_hbm,
    out,
    cuts, time, taper, chan, twist,
    recv, spec, coef, block, below, above, limit, lines_time,
    own, spill_low, spill_high, low_in, high_in, arrived, turned, stage_back,
    load_sem, cut_send, cut_sem,
    rows_send, ring_recv, wave_send, wave_recv, halo_send, halo_recv,
    spill_send, spill_recv, lines_send, lines_recv, home_send, home_recv, last_send, last_recv,
):
    tm = lax.axis_index("tm")
    chan_index = lax.axis_index("chan")
    zed, side = div(chan_index, 2), rem(chan_index, 2)
    place = 2 * tm + side

    def in_plane(other):
        return {"tm": div(other, 2), "chan": 2 * zed + rem(other, 2)}

    def in_ring(other):
        return {"chan": 2 * other + side}

    up = rem(zed + 1, RING)
    down = rem(zed + RING - 1, RING)

    loads = [pltpu.make_async_copy(taper_hbm, taper, load_sem.at[0])]
    loads += [
        pltpu.make_async_copy(chan_hbm, chan, load_sem.at[1]),
        pltpu.make_async_copy(twist_hbm, twist, load_sem.at[2]),
        pltpu.make_async_copy(time_hbm, time, load_sem.at[3]),
    ]

    def piece(other, chunk):
        return record_hbm.at[pl.ds(pl.multiple_of(32 * other + ROWS * chunk, ROWS), ROWS)]

    barrier = pltpu.get_barrier_semaphore()

    for step in range(1, GROUPS):
        other = rem(place + 11 * step % GROUPS, GROUPS)
        pl.semaphore_signal(barrier, inc=1, device_id=in_plane(other), device_id_type=MESH_ID)

    for step in range(1, RING):
        other = rem(zed + 7 * step % RING, RING)
        pl.semaphore_signal(barrier, inc=1, device_id=in_ring(other), device_id_type=MESH_ID)

    @pl.loop(0, GROUPS)
    def _(step):
        pl.semaphore_signal(
            barrier, inc=1, device_id={"tm": zed, "chan": step}, device_id_type=MESH_ID
        )

    for load in loads:
        load.start()

    pl.semaphore_wait(barrier, 2 * GROUPS + RING - 2)

    def remote(source, target, send_sem, recv_sem, device):
        return pltpu.make_async_remote_copy(
            src_ref=source, dst_ref=target, send_sem=send_sem, recv_sem=recv_sem,
            device_id=device, device_id_type=MESH_ID,
        )

    def plane_exchange(source_of, target, send_sem, recv_sem):
        for step in range(1, GROUPS):
            other = rem(place + 11 * step % GROUPS, GROUPS)
            remote(source_of(other), target, send_sem, recv_sem, in_plane(other)).start()

    def ring_exchange(source, target, chunk, send_sem, recv_sem):
        for step in range(1, RING):
            other = rem(zed + 7 * step % RING, RING)
            remote(
                source.at[chunk, pl.ds(2 * other, 2)], target.at[chunk, pl.ds(2 * zed, 2)],
                send_sem.at[chunk], recv_sem.at[chunk], in_ring(other),
            ).start()

        for i in range(2):
            target[chunk, 2 * zed + i] = source[chunk, 2 * zed + i]

    def bytes_of(buffer, count, sem):
        span = buffer.at[0, pl.ds(0, count)]
        return pltpu.make_async_copy(span, span, sem)

    def plane_wait(sem):
        bytes_of(recv, GROUPS - 1, sem).wait()

    def ring_wait(sem):
        bytes_of(recv, GROUPS - 2, sem).wait()

    for c in range(CHUNKS):
        @pl.loop(0, GROUPS)
        def _(step):
            other = rem(place + 11 * step, GROUPS)
            target = recv.at[c, chan_index]

            @pl.when(jnp.logical_or(tm != zed, step != 0))
            def _():
                where = {"tm": div(other, 2), "chan": 2 * tm + rem(other, 2)}
                remote(piece(other, c), target, rows_send.at[c], ring_recv.at[c], where).start()

            @pl.when(jnp.logical_and(tm == zed, step == 0))
            def _():
                pltpu.make_async_copy(piece(other, c), target, ring_recv.at[c]).start()

    @pl.when(tm == zed)
    def _():
        @pl.loop(1, RING)
        def _(step):
            other = rem(tm + step, RING)
            remote(cuts_hbm, cuts, cut_send.at[step], cut_sem.at[0], {"tm": other}).start()

        copy = pltpu.make_async_copy(cuts_hbm, cuts, cut_sem.at[1])
        copy.start()
        copy.wait()

    @pl.when(tm != zed)
    def _():
        remote(cuts_hbm, cuts, cut_send.at[0], cut_sem.at[0], {"tm": zed}).wait_recv()

    for p in range(TIMES):
        @pl.loop(0, 8)
        def _(j):
            row = 32 * j + lax.broadcasted_iota(jnp.int32, (32, 1), 0)
            if p == 0:
                freq = jnp.where(row < LANES, TALL * row, TALL * (row - LANES) + TIMES)
            else:
                freq = p + TALL * jnp.where(row < LANES, row, row - LANES)
            band = jnp.minimum(jnp.minimum(freq, WIN - freq), HOP - 1)
            total = jnp.zeros((32, LANES), jnp.int32)
            for i in range(HOP // LANES):
                here = i * LANES + lax.broadcasted_iota(jnp.int32, (32, LANES), 1)
                total = total + jnp.where(here == band, cuts[0:1, i * LANES : (i + 1) * LANES], 0)
            total = jnp.sum(total, axis=1, keepdims=True)
            rows = pl.ds(pl.multiple_of(j * 32, 32), 32)
            limit[p, rows] = jnp.broadcast_to(total, (32, LANES))

    for load in loads:
        load.wait()

    whole = 2 * LANES
    keep_low = jnp.where(zed > 0, 1.0, 0.0).astype(jnp.float32)
    keep_high = jnp.where(zed < RING - 1, 1.0, 0.0).astype(jnp.float32)

    halos = []

    def start_halo(c):
        plane_wait(wave_recv.at[c])
        halos.extend([
            remote(
                block.at[c, pl.ds(HALF, HALF)], below.at[c],
                halo_send.at[2 * c], halo_recv.at[2 * c], in_ring(up),
            ),
            remote(
                block.at[c, pl.ds(0, HALF)], above.at[c],
                halo_send.at[2 * c + 1], halo_recv.at[2 * c + 1], in_ring(down),
            ),
        ])
        for halo in halos[-2:]:
            halo.start()

    quarter = TALL // 4

    def fold(c):
        for halo in halos[2 * c : 2 * c + 2]:
            halo.wait_recv()

        @pl.loop(0, 4)
        def _(a):
            start = 32 * a + ROWS * c
            cells = []
            for i in range(TALL):
                weight = taper[pl.ds(pl.multiple_of(LANES * i + start, 8), ROWS)]
                if i < quarter:
                    cells.append(below[c, 4 * i + a] * (weight * keep_low))
                elif i < 3 * quarter:
                    cells.append(block[c, 4 * (i - quarter) + a] * weight)
                else:
                    cells.append(above[c, 4 * (i - 3 * quarter) + a] * (weight * keep_high))
            here = pl.ds(pl.multiple_of(start, 8), ROWS)
            there = pl.ds(pl.multiple_of(LANES + start, 8), ROWS)
            for p, (re, im) in enumerate(real_dft(cells)):
                if p == TIMES:
                    lines_time[0, there] = re
                else:
                    lines_time[p, here] = re
                    if p > 0:
                        lines_time[p, there] = im

    for c in range(CHUNKS):
        bytes_of(recv, GROUPS, ring_recv.at[c]).wait()

        @pl.loop(0, ROWS // 8)
        def _(i):
            rows = pl.ds(pl.multiple_of(i * 8, 8), 8)
            lines = real_dft([recv[c, d, rows] for d in range(GROUPS)])
            for p, (re, im) in enumerate(lines):
                if p == 0:
                    spec[p, rows, 0:LANES] = re
                    spec[p, rows, LANES:whole] = jnp.zeros_like(re)
                elif im is None:
                    spec[p, rows, 0:LANES] = re * twist[0, p]
                    spec[p, rows, LANES:whole] = -(re * twist[1, p])
                else:
                    cosine, sine = twist[0, p], twist[1, p]
                    spec[p, rows, 0:LANES] = re * cosine + im * sine
                    spec[p, rows, LANES:whole] = im * cosine - re * sine

        lines = spec[...].reshape(PARTS * ROWS, whole)
        lines = table_product(lines, chan[0], chan[1]).reshape(PARTS, ROWS, whole)
        for p in range(PARTS):
            re, im = lines[p, :, 0:LANES], lines[p, :, LANES:whole]
            if p == 0:
                coef[c, 0] = re - im
            elif p == PARTS - 1:
                coef[c, GROUPS - 1] = re - im
            else:
                coef[c, 2 * p - 1] = re
                coef[c, 2 * p] = im

        plane_exchange(
            lambda other: coef.at[c, other], block.at[c, place], wave_send.at[c], wave_recv.at[c]
        )
        block[c, place] = coef[c, place]
        if c > 0:
            start_halo(c - 1)
        if c > 1:
            fold(c - 2)

    start_halo(CHUNKS - 1)
    fold(CHUNKS - 2)
    fold(CHUNKS - 1)

    lane = lax.broadcasted_iota(jnp.int32, (1, LANES), 1)
    wave = div(place + 1, 2) + GROUPS * lane
    wave = jnp.minimum(wave, NCH - wave)

    def time_product(way, p, values):
        high, low = halves(values)
        wide = dot(time[way, p], jnp.concatenate([high, low], axis=1))
        main, rest = wide[0:whole], wide[whole : 2 * whole]
        return (main[:, LANES:whole] + rest[:, 0:LANES]) + (rest[:, LANES:whole] + main[:, 0:LANES])

    for p in range(TIMES):
        values = time_product(0, p, lines_time[p])
        lines_time[p] = time_product(1, p, jnp.where(wave <= limit[p], values, 0.0))

    per = LANES // ROWS

    @pl.loop(0, per)
    def _(g):
        here = pl.ds(pl.multiple_of(ROWS * g, ROWS), ROWS)
        there = pl.ds(pl.multiple_of(LANES + ROWS * g, ROWS), ROWS)
        lines = [(lines_time[0, here], None)]
        for p in range(1, TIMES):
            lines.append((lines_time[p, here], lines_time[p, there]))
        lines.append((lines_time[0, there], None))
        for i, value in enumerate(real_inverse(lines)):
            weight = taper[pl.ds(pl.multiple_of(LANES * i + ROWS * g, ROWS), ROWS)]
            value = value * weight
            if i < quarter:
                target, k = spill_low, i
            elif i < 3 * quarter:
                target, k = own, i - quarter
            else:
                target, k = spill_high, i - 3 * quarter
            target[k // PER_CHUNK, per * (k % PER_CHUNK) + g] = value

    spills = {}
    order = [c for pair in zip(range(CHUNKS // 2), range(CHUNKS // 2, CHUNKS)) for c in pair]
    for c in order:
        k = c % (CHUNKS // 2)
        if c < CHUNKS // 2:
            source, target, other = spill_high.at[k], high_in.at[k], up
        else:
            source, target, other = spill_low.at[k], low_in.at[k], down
        spills[c] = remote(source, target, spill_send.at[c], spill_recv.at[c], in_ring(other))
        spills[c].start()

    def send_lines(c):
        spills[c].wait_recv()
        extra, keep = (high_in, keep_low) if c < CHUNKS // 2 else (low_in, keep_high)

        @pl.loop(0, GROUPS)
        def _(q):
            own[c, q] = own[c, q] + extra[c % (CHUNKS // 2), q] * keep

        plane_exchange(
            lambda other: own.at[c, other], arrived.at[c, place], lines_send.at[c], lines_recv.at[c]
        )
        arrived[c, place] = own[c, place]

    send_lines(order[0])
    for step, c in enumerate(order):
        if step + 1 < CHUNKS:
            send_lines(order[step + 1])
        plane_wait(lines_recv.at[c])
        for p in range(PARTS):
            if p == 0 or p == PARTS - 1:
                re = arrived[c, 0 if p == 0 else GROUPS - 1]
                im = -re
            else:
                re, im = arrived[c, 2 * p - 1], arrived[c, 2 * p]
            spec[p, :, 0:LANES] = re
            spec[p, :, LANES:whole] = im
        lines = spec[...].reshape(PARTS * ROWS, whole)
        spec[...] = table_product(lines, chan[2], chan[3]).reshape(PARTS, ROWS, whole)

        @pl.loop(0, ROWS // 8)
        def _(i):
            rows = pl.ds(pl.multiple_of(i * 8, 8), 8)
            lines = []
            for p in range(PARTS):
                re, im = spec[p, rows, 0:LANES], spec[p, rows, LANES:whole]
                cosine, sine = twist[0, p], twist[1, p]
                if p == 0:
                    lines.append((re, None))
                elif p == PARTS - 1:
                    lines.append((re * cosine - im * sine, None))
                else:
                    lines.append((re * cosine - im * sine, im * cosine + re * sine))
            for d, value in enumerate(real_inverse(lines)):
                turned[c, d, rows] = value

        ring_exchange(turned, stage_back, c, home_send, home_recv)

    def final(c):
        return pl.ds(pl.multiple_of(HOP // CHUNKS * c + ROWS * place, ROWS), ROWS)

    for c in order:
        ring_wait(home_recv.at[c])
        plane_exchange(
            lambda other: stage_back.at[c, other], out.at[final(c)], last_send.at[c], last_recv.at[c]
        )
        out[final(c)] = stage_back[c, place]

    for c in range(CHUNKS):
        plane_wait(last_recv.at[c])
    for c in range(CHUNKS):
        for sem in (wave_send, lines_send, last_send):
            plane_wait(sem.at[c])
        ring_wait(home_send.at[c])

        @pl.when(tm == zed)
        def _():
            bytes_of(recv, GROUPS - 1, rows_send.at[c]).wait()

        @pl.when(tm != zed)
        def _():
            bytes_of(recv, GROUPS, rows_send.at[c]).wait()
    for copy in halos + list(spills.values()):
        copy.wait_send()

    @pl.when(tm == zed)
    def _():
        @pl.loop(1, RING)
        def _(step):
            other = rem(tm + step, RING)
            remote(cuts_hbm, cuts, cut_send.at[step], cut_sem.at[0], {"tm": other}).wait_send()


def per_device(record, cuts):
    time, taper, chan, twist = tables()
    blocks = pltpu.VMEM((CHUNKS, GROUPS, ROWS, LANES), jnp.float32)
    half = pltpu.VMEM((CHUNKS, HALF, ROWS, LANES), jnp.float32)
    rim = pltpu.VMEM((CHUNKS // 2, GROUPS, ROWS, LANES), jnp.float32)
    dma = pltpu.SemaphoreType.DMA
    result = pl.pallas_call(
        body,
        out_shape=jax.ShapeDtypeStruct(record.shape, jnp.float32),
        in_specs=[pl.BlockSpec(memory_space=pltpu.HBM)] * 6,
        out_specs=pl.BlockSpec(memory_space=pltpu.VMEM),
        scratch_shapes=[
            pltpu.VMEM(cuts.shape, jnp.int32),
            pltpu.VMEM(time.shape, jnp.bfloat16),
            pltpu.VMEM(taper.shape, jnp.float32),
            pltpu.VMEM(chan.shape, jnp.bfloat16),
            pltpu.VMEM(twist.shape, jnp.float32),
            blocks,
            pltpu.VMEM((PARTS, ROWS, 2 * LANES), jnp.float32),
            blocks, blocks, half, half,
            pltpu.VMEM((TIMES, 2 * LANES, LANES), jnp.int32),
            pltpu.VMEM((TIMES, 2 * LANES, LANES), jnp.float32),
            blocks, rim, rim, rim, rim, blocks, blocks, blocks,
            dma((4,)), dma((RING,)), dma((2,)),
            *[dma((CHUNKS,))] * 4, *[dma((2 * CHUNKS,))] * 2, *[dma((CHUNKS,))] * 8,
        ],
        compiler_params=pltpu.CompilerParams(
            collective_id=0, has_side_effects=True, vmem_limit_bytes=60 * 1024 * 1024
        ),
    )(record, cuts, time, taper, chan, twist)
    return result * (1.0 / (WIN * NCH))


def solution(mesh):
    return jax.shard_map(
        per_device,
        mesh=mesh,
        in_specs=(P("tm", "chan"), P("tm", None)),
        out_specs=P("tm", "chan"),
        check_vma=False,
    )
```

```python
import functools
import math

import jax
import jax.numpy as jnp
import ml_dtypes
import numpy as np
from jax import lax
from jax.experimental import pallas as pl
from jax.experimental.pallas import tpu as pltpu
from jax.sharding import PartitionSpec as P

WIN = 2048
HOP = WIN // 2
RIM = HOP // 2
NCH = 4096
GROUPS = 32
LANES = 128
RING = 16
PARTS = 17
CHUNKS = 4
ROWS = 32 // CHUNKS
HALF = GROUPS // 2
TALL = WIN // LANES
TIMES = TALL // 2
PER_CHUNK = 8 // CHUNKS
MESH_ID = pl.DeviceIdType.MESH


def split_bf16(table):
    high = table.astype(np.float32).astype(ml_dtypes.bfloat16)
    low = (table - high.astype(np.float64)).astype(ml_dtypes.bfloat16)
    return np.stack([high, low])


def cas(angle):
    return np.cos(angle) + np.sin(angle)


@functools.cache
def tables():
    point = np.arange(LANES)
    blocks = []
    for p in range(TIMES):
        freq = p + TALL * point
        angle = 2.0 * np.pi / WIN * (np.outer(freq, point) % WIN)
        cosine, sine = np.cos(angle), np.sin(angle)
        if p == 0:
            middle = 2.0 * np.pi / WIN * (np.outer(TIMES + freq, point) % WIN)
            none = np.zeros_like(angle)
            blocks.append(np.block([[cas(angle), none], [none, cas(middle)]]))
        else:
            blocks.append(np.block([[cosine, sine], [-sine, cosine]]))
    blocks = np.stack(blocks)
    time = np.stack([split_bf16(blocks), split_bf16(blocks.transpose(0, 2, 1))])
    time = time.transpose(0, 2, 1, 3, 4).reshape(2, TIMES, 4 * LANES, 2 * LANES)
    taper = np.sin(np.pi / WIN * np.arange(WIN)) ** 2
    taper = np.repeat(taper[:, None], LANES, axis=1).astype(np.float32)
    lane = np.arange(LANES)
    angle = 2.0 * np.pi / LANES * (np.outer(lane, lane) % LANES)
    cosine, sine = np.cos(angle), np.sin(angle)
    forward = np.block([[cosine, -sine], [sine, cosine]])
    inverse = np.block([[cosine, sine], [-sine, cosine]])
    chan = np.concatenate([split_bf16(forward), split_bf16(inverse)])
    angle = 2.0 * np.pi / NCH * np.outer(np.arange(PARTS), lane)
    twist = np.stack([np.cos(angle), np.sin(angle)]).astype(np.float32)
    twist = np.repeat(twist[:, :, None, :], 8, axis=2)
    return time, taper, chan, twist


def real_dft(x):
    n = len(x)
    if n == 1:
        return [(x[0], None)]
    if n == 2:
        return [(x[0] + x[1], None), (x[0] - x[1], None)]
    even = real_dft(x[0::2])
    odd = real_dft(x[1::2])
    half = n // 2
    out = [None] * (half + 1)
    out[0] = (even[0][0] + odd[0][0], None)
    out[half] = (even[0][0] - odd[0][0], None)
    for k in range(1, half // 2 + 1):
        e_re, e_im = even[k]
        o_re, o_im = odd[k]
        if 2 * k == half:
            out[k] = (e_re, -o_re)
            continue
        c, s = math.cos(2.0 * math.pi * k / n), math.sin(2.0 * math.pi * k / n)
        t_re = c * o_re + s * o_im
        t_im = c * o_im - s * o_re
        out[k] = (e_re + t_re, e_im + t_im)
        out[half - k] = (e_re - t_re, t_im - e_im)
    return out


def real_inverse(spec):
    half = len(spec) - 1
    n = 2 * half
    first, last = spec[0][0], spec[half][0]
    if n == 2:
        return [first + last, first - last]
    even = [None] * (half // 2 + 1)
    odd = [None] * (half // 2 + 1)
    even[0] = (first + last, None)
    odd[0] = (first - last, None)
    for k in range(1, half // 2 + 1):
        a_re, a_im = spec[k]
        if 2 * k == half:
            even[k] = (2.0 * a_re, None)
            odd[k] = (-2.0 * a_im, None)
            continue
        b_re, b_im = spec[half - k]
        even[k] = (a_re + b_re, a_im - b_im)
        d_re, d_im = a_re - b_re, a_im + b_im
        c, s = math.cos(2.0 * math.pi * k / n), math.sin(2.0 * math.pi * k / n)
        odd[k] = (c * d_re - s * d_im, c * d_im + s * d_re)
    y_even = real_inverse(even)
    y_odd = real_inverse(odd)
    out = []
    for a, b in zip(y_even, y_odd):
        out += [a, b]
    return out


def dot(a, b):
    return jnp.dot(a, b, preferred_element_type=jnp.float32)


def halves(x):
    high = x.astype(jnp.bfloat16)
    low = (x - high.astype(jnp.float32)).astype(jnp.bfloat16)
    return high, low


def table_product(x, high_table, low_table):
    high, low = halves(x)
    return dot(high, high_table) + dot(high, low_table) + dot(low, high_table)


def div(a, b):
    return lax.div(a, jnp.int32(b))


def rem(a, b):
    return lax.rem(a, jnp.int32(b))


def body(
    record_hbm, cuts_hbm, time_hbm, taper_hbm, chan_hbm, twist_hbm,
    out,
    cuts, time, taper, chan, twist,
    stage, recv, spec, coef, block, below, above, limit, lines_time,
    own, spill_low, spill_high, low_in, high_in, arrived, turned,
    load_sem, cut_send, cut_sem,
    rows_send, rows_recv, ring_send, ring_recv, wave_send, wave_recv, halo_send, halo_recv,
    spill_send, spill_recv, lines_send, lines_recv, last_send, last_recv,
):
    tm = lax.axis_index("tm")
    chan_index = lax.axis_index("chan")
    zed, side = div(chan_index, 2), rem(chan_index, 2)
    place = 2 * tm + side

    def in_plane(other):
        return {"tm": div(other, 2), "chan": 2 * zed + rem(other, 2)}

    def in_ring(other):
        return {"chan": 2 * other + side}

    up = rem(zed + 1, RING)
    down = rem(zed + RING - 1, RING)

    loads = [pltpu.make_async_copy(taper_hbm, taper, load_sem.at[0])]
    loads += [
        pltpu.make_async_copy(chan_hbm, chan, load_sem.at[1]),
        pltpu.make_async_copy(twist_hbm, twist, load_sem.at[2]),
        pltpu.make_async_copy(time_hbm, time, load_sem.at[3]),
    ]

    def piece(other, chunk):
        return record_hbm.at[pl.ds(pl.multiple_of(32 * other + ROWS * chunk, ROWS), ROWS)]

    mine = [
        pltpu.make_async_copy(piece(place, c), stage.at[c, place], load_sem.at[4 + c])
        for c in range(CHUNKS)
    ]

    barrier = pltpu.get_barrier_semaphore()

    for step in range(1, GROUPS):
        other = rem(place + 11 * step % GROUPS, GROUPS)
        pl.semaphore_signal(barrier, inc=1, device_id=in_plane(other), device_id_type=MESH_ID)

    for step in range(1, RING):
        other = rem(zed + 7 * step % RING, RING)
        pl.semaphore_signal(barrier, inc=1, device_id=in_ring(other), device_id_type=MESH_ID)

    @pl.loop(0, GROUPS)
    def _(step):
        where = {"tm": div(step, 2), "chan": 2 * tm + rem(step, 2)}
        pl.semaphore_signal(barrier, inc=1, device_id=where, device_id_type=MESH_ID)

    for load in mine + loads:
        load.start()

    pl.semaphore_wait(barrier, 2 * GROUPS + RING - 2)

    def remote(source, target, send_sem, recv_sem, device):
        return pltpu.make_async_remote_copy(
            src_ref=source, dst_ref=target, send_sem=send_sem, recv_sem=recv_sem,
            device_id=device, device_id_type=MESH_ID,
        )

    def plane_exchange(source_of, target, send_sem, recv_sem):
        for step in range(1, GROUPS):
            other = rem(place + 11 * step % GROUPS, GROUPS)
            remote(source_of(other), target, send_sem, recv_sem, in_plane(other)).start()

    def ring_exchange(source, target, chunk, send_sem, recv_sem):
        for step in range(1, RING):
            other = rem(zed + 7 * step % RING, RING)
            remote(
                source.at[chunk, pl.ds(2 * other, 2)], target.at[chunk, pl.ds(2 * zed, 2)],
                send_sem.at[chunk], recv_sem.at[chunk], in_ring(other),
            ).start()

        for i in range(2):
            target[chunk, 2 * zed + i] = source[chunk, 2 * zed + i]

    def bytes_of(buffer, count, sem):
        span = buffer.at[0, pl.ds(0, count)]
        return pltpu.make_async_copy(span, span, sem)

    def plane_wait(sem):
        bytes_of(recv, GROUPS - 1, sem).wait()

    def ring_wait(sem):
        bytes_of(recv, GROUPS - 2, sem).wait()

    def send_rows(c):
        plane_exchange(
            lambda other: piece(other, c), stage.at[c, place], rows_send.at[c], rows_recv.at[c]
        )

    send_rows(0)

    @pl.when(tm == zed)
    def _():
        @pl.loop(1, RING)
        def _(step):
            other = rem(tm + step, RING)
            remote(cuts_hbm, cuts, cut_send.at[step], cut_sem.at[0], {"tm": other}).start()

        copy = pltpu.make_async_copy(cuts_hbm, cuts, cut_sem.at[1])
        copy.start()
        copy.wait()

    for c in range(CHUNKS):
        if c + 1 < CHUNKS:
            send_rows(c + 1)
        mine[c].wait()
        plane_wait(rows_recv.at[c])
        ring_exchange(stage, recv, c, ring_send, ring_recv)

    @pl.when(tm != zed)
    def _():
        remote(cuts_hbm, cuts, cut_send.at[0], cut_sem.at[0], {"tm": zed}).wait_recv()

    for p in range(TIMES):
        @pl.loop(0, 8)
        def _(j):
            row = 32 * j + lax.broadcasted_iota(jnp.int32, (32, 1), 0)
            if p == 0:
                freq = jnp.where(row < LANES, TALL * row, TALL * (row - LANES) + TIMES)
            else:
                freq = p + TALL * jnp.where(row < LANES, row, row - LANES)
            band = jnp.minimum(jnp.minimum(freq, WIN - freq), HOP - 1)
            total = jnp.zeros((32, LANES), jnp.int32)
            for i in range(HOP // LANES):
                here = i * LANES + lax.broadcasted_iota(jnp.int32, (32, LANES), 1)
                total = total + jnp.where(here == band, cuts[0:1, i * LANES : (i + 1) * LANES], 0)
            total = jnp.sum(total, axis=1, keepdims=True)
            rows = pl.ds(pl.multiple_of(j * 32, 32), 32)
            limit[p, rows] = jnp.broadcast_to(total, (32, LANES))

    for load in loads:
        load.wait()

    whole = 2 * LANES
    keep_low = jnp.where(zed > 0, 1.0, 0.0).astype(jnp.float32)
    keep_high = jnp.where(zed < RING - 1, 1.0, 0.0).astype(jnp.float32)

    halos = []

    def start_halo(c):
        plane_wait(wave_recv.at[c])
        halos.extend([
            remote(
                block.at[c, pl.ds(HALF, HALF)], below.at[c],
                halo_send.at[2 * c], halo_recv.at[2 * c], in_ring(up),
            ),
            remote(
                block.at[c, pl.ds(0, HALF)], above.at[c],
                halo_send.at[2 * c + 1], halo_recv.at[2 * c + 1], in_ring(down),
            ),
        ])
        for halo in halos[-2:]:
            halo.start()

    quarter = TALL // 4

    def fold(c):
        for halo in halos[2 * c : 2 * c + 2]:
            halo.wait_recv()

        @pl.loop(0, 4)
        def _(a):
            start = 32 * a + ROWS * c
            cells = []
            for i in range(TALL):
                weight = taper[pl.ds(pl.multiple_of(LANES * i + start, 8), ROWS)]
                if i < quarter:
                    cells.append(below[c, 4 * i + a] * (weight * keep_low))
                elif i < 3 * quarter:
                    cells.append(block[c, 4 * (i - quarter) + a] * weight)
                else:
                    cells.append(above[c, 4 * (i - 3 * quarter) + a] * (weight * keep_high))
            here = pl.ds(pl.multiple_of(start, 8), ROWS)
            there = pl.ds(pl.multiple_of(LANES + start, 8), ROWS)
            for p, (re, im) in enumerate(real_dft(cells)):
                if p == TIMES:
                    lines_time[0, there] = re
                else:
                    lines_time[p, here] = re
                    if p > 0:
                        lines_time[p, there] = im

    for c in range(CHUNKS):
        ring_wait(ring_recv.at[c])

        @pl.loop(0, ROWS // 8)
        def _(i):
            rows = pl.ds(pl.multiple_of(i * 8, 8), 8)
            lines = real_dft([recv[c, d, rows] for d in range(GROUPS)])
            for p, (re, im) in enumerate(lines):
                if p == 0:
                    spec[p, rows, 0:LANES] = re
                    spec[p, rows, LANES:whole] = jnp.zeros_like(re)
                elif im is None:
                    spec[p, rows, 0:LANES] = re * twist[0, p]
                    spec[p, rows, LANES:whole] = -(re * twist[1, p])
                else:
                    cosine, sine = twist[0, p], twist[1, p]
                    spec[p, rows, 0:LANES] = re * cosine + im * sine
                    spec[p, rows, LANES:whole] = im * cosine - re * sine

        lines = spec[...].reshape(PARTS * ROWS, whole)
        lines = table_product(lines, chan[0], chan[1]).reshape(PARTS, ROWS, whole)
        for p in range(PARTS):
            re, im = lines[p, :, 0:LANES], lines[p, :, LANES:whole]
            if p == 0:
                coef[c, 0] = re - im
            elif p == PARTS - 1:
                coef[c, GROUPS - 1] = re - im
            else:
                coef[c, 2 * p - 1] = re
                coef[c, 2 * p] = im

        plane_exchange(
            lambda other: coef.at[c, other], block.at[c, place], wave_send.at[c], wave_recv.at[c]
        )
        block[c, place] = coef[c, place]
        if c > 0:
            start_halo(c - 1)
        if c > 1:
            fold(c - 2)

    start_halo(CHUNKS - 1)
    fold(CHUNKS - 2)
    fold(CHUNKS - 1)

    lane = lax.broadcasted_iota(jnp.int32, (1, LANES), 1)
    wave = div(place + 1, 2) + GROUPS * lane
    wave = jnp.minimum(wave, NCH - wave)

    def time_product(way, p, values):
        high, low = halves(values)
        wide = dot(time[way, p], jnp.concatenate([high, low], axis=1))
        main, rest = wide[0:whole], wide[whole : 2 * whole]
        return (main[:, LANES:whole] + rest[:, 0:LANES]) + (rest[:, LANES:whole] + main[:, 0:LANES])

    for p in range(TIMES):
        values = time_product(0, p, lines_time[p])
        lines_time[p] = time_product(1, p, jnp.where(wave <= limit[p], values, 0.0))

    per = LANES // ROWS

    @pl.loop(0, per)
    def _(g):
        here = pl.ds(pl.multiple_of(ROWS * g, ROWS), ROWS)
        there = pl.ds(pl.multiple_of(LANES + ROWS * g, ROWS), ROWS)
        lines = [(lines_time[0, here], None)]
        for p in range(1, TIMES):
            lines.append((lines_time[p, here], lines_time[p, there]))
        lines.append((lines_time[0, there], None))
        for i, value in enumerate(real_inverse(lines)):
            weight = taper[pl.ds(pl.multiple_of(LANES * i + ROWS * g, ROWS), ROWS)]
            value = value * weight
            if i < quarter:
                target, k = spill_low, i
            elif i < 3 * quarter:
                target, k = own, i - quarter
            else:
                target, k = spill_high, i - 3 * quarter
            target[k // PER_CHUNK, per * (k % PER_CHUNK) + g] = value

    spills = {}
    order = [c for pair in zip(range(CHUNKS // 2), range(CHUNKS // 2, CHUNKS)) for c in pair]
    for c in order:
        k = c % (CHUNKS // 2)
        if c < CHUNKS // 2:
            source, target, other = spill_high.at[k], high_in.at[k], up
        else:
            source, target, other = spill_low.at[k], low_in.at[k], down
        spills[c] = remote(source, target, spill_send.at[c], spill_recv.at[c], in_ring(other))
        spills[c].start()

    def send_lines(c):
        spills[c].wait_recv()
        extra, keep = (high_in, keep_low) if c < CHUNKS // 2 else (low_in, keep_high)

        @pl.loop(0, GROUPS)
        def _(q):
            own[c, q] = own[c, q] + extra[c % (CHUNKS // 2), q] * keep

        plane_exchange(
            lambda other: own.at[c, other], arrived.at[c, place], lines_send.at[c], lines_recv.at[c]
        )
        arrived[c, place] = own[c, place]

    send_lines(order[0])
    for step, c in enumerate(order):
        if step + 1 < CHUNKS:
            send_lines(order[step + 1])
        plane_wait(lines_recv.at[c])
        for p in range(PARTS):
            if p == 0 or p == PARTS - 1:
                re = arrived[c, 0 if p == 0 else GROUPS - 1]
                im = -re
            else:
                re, im = arrived[c, 2 * p - 1], arrived[c, 2 * p]
            spec[p, :, 0:LANES] = re
            spec[p, :, LANES:whole] = im
        lines = spec[...].reshape(PARTS * ROWS, whole)
        spec[...] = table_product(lines, chan[2], chan[3]).reshape(PARTS, ROWS, whole)

        @pl.loop(0, ROWS // 8)
        def _(i):
            rows = pl.ds(pl.multiple_of(i * 8, 8), 8)
            lines = []
            for p in range(PARTS):
                re, im = spec[p, rows, 0:LANES], spec[p, rows, LANES:whole]
                cosine, sine = twist[0, p], twist[1, p]
                if p == 0:
                    lines.append((re, None))
                elif p == PARTS - 1:
                    lines.append((re * cosine - im * sine, None))
                else:
                    lines.append((re * cosine - im * sine, im * cosine + re * sine))
            for d, value in enumerate(real_inverse(lines)):
                turned[c, d, rows] = value

        final = pl.ds(pl.multiple_of(HOP // CHUNKS * c + ROWS * place, ROWS), ROWS)

        @pl.loop(0, GROUPS)
        def _(hop):
            other = rem(chan_index + 11 * hop, GROUPS)
            source, target = turned.at[c, other], out.at[final]

            @pl.when(jnp.logical_or(tm != zed, hop != 0))
            def _():
                where = {"tm": zed, "chan": other}
                remote(source, target, last_send.at[c], last_recv.at[c], where).start()

            @pl.when(jnp.logical_and(tm == zed, hop == 0))
            def _():
                pltpu.make_async_copy(source, target, last_recv.at[c]).start()

    for c in range(CHUNKS):
        bytes_of(recv, GROUPS, last_recv.at[c]).wait()
    for c in range(CHUNKS):
        for sem in (rows_send, wave_send, lines_send):
            plane_wait(sem.at[c])
        ring_wait(ring_send.at[c])

        @pl.when(tm == zed)
        def _():
            bytes_of(recv, GROUPS - 1, last_send.at[c]).wait()

        @pl.when(tm != zed)
        def _():
            bytes_of(recv, GROUPS, last_send.at[c]).wait()
    for copy in halos + list(spills.values()):
        copy.wait_send()

    @pl.when(tm == zed)
    def _():
        @pl.loop(1, RING)
        def _(step):
            other = rem(tm + step, RING)
            remote(cuts_hbm, cuts, cut_send.at[step], cut_sem.at[0], {"tm": other}).wait_send()


def per_device(record, cuts):
    time, taper, chan, twist = tables()
    blocks = pltpu.VMEM((CHUNKS, GROUPS, ROWS, LANES), jnp.float32)
    half = pltpu.VMEM((CHUNKS, HALF, ROWS, LANES), jnp.float32)
    rim = pltpu.VMEM((CHUNKS // 2, GROUPS, ROWS, LANES), jnp.float32)
    dma = pltpu.SemaphoreType.DMA
    result = pl.pallas_call(
        body,
        out_shape=jax.ShapeDtypeStruct(record.shape, jnp.float32),
        in_specs=[pl.BlockSpec(memory_space=pltpu.HBM)] * 6,
        out_specs=pl.BlockSpec(memory_space=pltpu.VMEM),
        scratch_shapes=[
            pltpu.VMEM(cuts.shape, jnp.int32),
            pltpu.VMEM(time.shape, jnp.bfloat16),
            pltpu.VMEM(taper.shape, jnp.float32),
            pltpu.VMEM(chan.shape, jnp.bfloat16),
            pltpu.VMEM(twist.shape, jnp.float32),
            blocks, blocks,
            pltpu.VMEM((PARTS, ROWS, 2 * LANES), jnp.float32),
            blocks, blocks, half, half,
            pltpu.VMEM((TIMES, 2 * LANES, LANES), jnp.int32),
            pltpu.VMEM((TIMES, 2 * LANES, LANES), jnp.float32),
            blocks, rim, rim, rim, rim, blocks, blocks,
            dma((4 + CHUNKS,)), dma((RING,)), dma((2,)),
            *[dma((CHUNKS,))] * 6, *[dma((2 * CHUNKS,))] * 2, *[dma((CHUNKS,))] * 6,
        ],
        compiler_params=pltpu.CompilerParams(
            collective_id=0, has_side_effects=True, vmem_limit_bytes=60 * 1024 * 1024
        ),
    )(record, cuts, time, taper, chan, twist)
    return result * (1.0 / (WIN * NCH))


def solution(mesh):
    return jax.shard_map(
        per_device,
        mesh=mesh,
        in_specs=(P("tm", "chan"), P("tm", None)),
        out_specs=P("tm", "chan"),
        check_vma=False,
    )
```
